128 devices in a mesh: dp: 16 (over z_lo, y, core), context: 2 (over z_hi), tensor: 4 (over x).
Axes of the slice: x: 4, y: 4, z: 4 (z_hi: 2, z_lo: 2; z = z_hi * 2 + z_lo), core: 2. Of those that a mesh axis runs over, the one named last changes fastest.
Arguments:
- tokens: bfloat16 [16, 1024, 1024], P('dp', ('context', 'tensor')), may hold values from -6 to 6
- ln1_gain: float32 [1024], replicated, may hold values from 0.5 to 1.5
- ln1_bias: float32 [1024], replicated, may hold values from -1 to 1
- qkv_weight: bfloat16 [3, 1024, 1024], P(None, 'dp', 'tensor'), may hold values from -0.25 to 0.25
- qv_bias: float32 [2, 1024], P(None, 'tensor'), may hold values from -1.5 to 1.5
- out_weight: bfloat16 [1024, 1024], P('tensor', 'dp'), may hold values from -1 to 1
- out_bias: float32 [1024], replicated, may hold values from -1 to 1
- ln2_gain: float32 [1024], replicated, may hold values from 0.5 to 1.5
- ln2_bias: float32 [1024], replicated, may hold values from -1 to 1
- fc_weight: bfloat16 [1024, 4096], P('dp', 'tensor'), may hold values from -0.1875 to 0.1875
- hidden_unit_bias: float32 [4096], P('tensor'), may hold values from -1.5 to 1.5
- proj_weight: bfloat16 [4096, 1024], P('tensor', 'dp'), may hold values from -0.125 to 0.125
- proj_bias: float32 [1024], replicated, may hold values from -1 to 1
- cotangent: bfloat16 [16, 1024, 1024], P('dp', ('context', 'tensor')), may hold values from -6 to 6
Outputs:
- output: bfloat16 [16, 1024, 1024], P('dp', ('context', 'tensor'))
- grad_tokens: bfloat16 [16, 1024, 1024], P('dp', ('context', 'tensor'))
- grad_ln1_gain: float32 [1024], replicated
- grad_ln1_bias: float32 [1024], replicated
- grad_qkv_weight: float32 [3, 1024, 1024], P(None, 'dp', 'tensor')
- grad_qv_bias: float32 [2, 1024], P(None, 'tensor')
- grad_out_weight: float32 [1024, 1024], P('tensor', 'dp')
- grad_out_bias: float32 [1024], replicated
- grad_ln2_gain: float32 [1024], replicated
- grad_ln2_bias: float32 [1024], replicated
- grad_fc_weight: float32 [1024, 4096], P('dp', 'tensor')
- grad_fc_bias: float32 [4096], P('tensor')
- grad_proj_weight: float32 [4096, 1024], P('tensor', 'dp')
- grad_proj_bias: float32 [1024], replicated
The draws below stay inside these ranges and needn't reach their ends.
All inputs are finite; a program needn't handle non-finite values.
Results may differ from the reference program's by a relative error of at most 0.025.
Values may be sent and summed in bfloat16 or wider, within the bound.
No kernel may reach another device: no remote copies, remote signals or barrier semaphores. Data moves between devices by JAX's collectives and lax.ppermute only.
A program may use at most 128 MiB of HBM per device.

```python
import math
import jax
import jax.numpy as jnp
from jax import lax

D = 1024
HEADS = 16
HEAD_DIM = 64
FF = 4096
LEN = 1024
SEQS = 16
BLOCK = 512


def raised(array, own_key, source, target, shards_of, factor):
    owner, partner = [(jnp.arange(array.shape[position]) // (array.shape[position] // shards_of)).reshape([-1 if axis == position else 1 for axis in range(array.ndim)]) for position in (source, target)]
    chosen = jax.random.permutation(own_key, shards_of)[partner]
    strong = (owner == chosen) | (owner == (partner + shards_of // 2) % shards_of)
    return jnp.where(strong, factor * array, array)


def levels(rng, extent, shards, smallest, top_value):
    level = 1.0
    for position, shards_of in shards:
        steps = jax.random.uniform(jax.random.fold_in(jax.random.fold_in(rng, 6), position), (shards_of,), jnp.float32, smallest / len(shards), top_value / len(shards))
        level = level * jnp.repeat(jnp.exp(steps), extent[position] // shards_of).reshape((-1,) + (1,) * (len(extent) - 1 - position))
    return level


def normal_values(key, dims, scale, limit, cuts=(), kind=jnp.bfloat16):
    factor_of = levels(key, dims, cuts, -0.22, 0.18) if cuts else 1.0
    drawn = jax.random.normal(key, dims, jnp.float32) * scale * factor_of
    return jnp.minimum(jnp.maximum(drawn, -limit), limit).astype(kind)


def bell_draw_with(rng, shape, scale, limit, split, heavy, kind=jnp.bfloat16):
    drawn = scale * jax.random.normal(rng, shape, jnp.float32)
    if split:
        drawn = drawn * levels(rng, shape, split, -0.22, 0.18)
    return jnp.clip(raised(drawn, jax.random.fold_in(rng, 3), *heavy), -limit, limit).astype(kind)


def setup_inputs(seed: int = 0) -> dict:
    seeds = jax.random.split(jax.random.key(seed), 15)
    return {
        "tokens": normal_values(seeds[0], (SEQS, LEN, D), 1.0, 6.0, ((0, 16), (1, 8))),
        "ln1_gain": jnp.clip(1.0 + 0.1 * jax.random.normal(seeds[1], (D,), jnp.float32), 0.5, 1.5),
        "ln1_bias": normal_values(seeds[2], (D,), 0.2, 1.0, (), jnp.float32),
        "qkv_weight": normal_values(seeds[3], (3, D, D), (D // 2) ** -0.5, 0.25, ((1, 16), (2, 4))),
        "qv_bias": normal_values(seeds[4], (2, D), 0.3, 1.5, ((1, 4),), jnp.float32),
        "out_weight": normal_values(seeds[5], (D, D), (D // 32) ** -0.5, 1.0, ((0, 4), (1, 16))),
        "out_bias": normal_values(seeds[6], (D,), 0.2, 1.0, (), jnp.float32),
        "ln2_gain": jnp.clip(1.0 + 0.1 * jax.random.normal(seeds[7], (D,), jnp.float32), 0.5, 1.5),
        "ln2_bias": normal_values(seeds[8], (D,), 0.2, 1.0, (), jnp.float32),
        "fc_weight": normal_values(seeds[9], (D, FF), D ** -0.5, 0.1875, ((0, 16), (1, 4))),
        "hidden_unit_bias": normal_values(seeds[10], (FF,), 0.3, 1.5, ((0, 4),), jnp.float32),
        "proj_weight": normal_values(seeds[11], (FF, D), (FF // 2) ** -0.5, 0.125, ((0, 4), (1, 16))),
        "proj_bias": normal_values(seeds[12], (D,), 0.2, 1.0, (), jnp.float32),
        "cotangent": bell_draw_with(seeds[13], (SEQS, LEN, D), 1.0, 6.0, ((0, 16), (1, 8)), (0, 2, 16, 2.0)),
    }


@jax.custom_vjp
def low(v):
    return lax.optimization_barrier(v.astype(jnp.bfloat16)).astype(jnp.float32)

@jax.custom_vjp
def low_back(v):
    return v

def low_keep(v):
    return (low(v), None)

def low_pass(kept, grad):
    return (grad,)

def back_keep(v):
    return (v, None)

def back_low(kept, grad):
    return (low(grad),)
low.defvjp(low_keep, low_pass)
low_back.defvjp(back_keep, back_low)

def matmul(left, right):
    return jnp.matmul(left, right, precision=lax.Precision.HIGHEST)

def layer_norm(values_in, norm_gain, norm_bias):
    average = lax.optimization_barrier(jnp.mean(values_in, axis=-1, keepdims=True))
    centred = values_in - average
    spread = lax.optimization_barrier(jnp.mean(centred * centred, axis=-1, keepdims=True))
    return centred * lax.rsqrt(spread + 1e-05) * norm_gain + norm_bias

def forward(params, inputs):
    ln1_gain, ln1_bias, qkv_weight, qv_bias, out_weight, out_bias, ln2_gain, ln2_bias, fc_weight, hidden_unit_bias, proj_weight, proj_bias = params
    packed, length, features = inputs.shape
    normed_one = low(layer_norm(inputs, ln1_gain, ln1_bias))
    queries = low(low_back(matmul(normed_one, qkv_weight[0]) + qv_bias[0]))
    key_states = low(low_back(matmul(normed_one, qkv_weight[1])))
    value_states = low(low_back(matmul(normed_one, qkv_weight[2]) + qv_bias[1]))
    queries = queries.reshape(packed, length, HEADS, HEAD_DIM)
    key_states = key_states.reshape(packed, length, HEADS, HEAD_DIM)
    value_states = value_states.reshape(packed, length, HEADS, HEAD_DIM)
    positions = jnp.arange(length, dtype=jnp.int32)
    scaling = HEAD_DIM ** (-0.5)

    def attend(block_index):
        offset = (block_index * BLOCK).astype(jnp.int32)
        row_block = lax.dynamic_slice_in_dim(queries, offset, BLOCK, 1)
        scores = low_back(jnp.einsum('pqhd,pkhd->phqk', row_block, key_states, precision=lax.Precision.HIGHEST) * scaling)
        places = offset + jnp.arange(BLOCK, dtype=jnp.int32)
        visible = places[:, None] >= positions[None, :]
        scores = jnp.where(visible, scores, -1e+30)
        weights = low(jax.nn.softmax(scores, axis=-1))
        return jnp.einsum('phqk,pkhd->pqhd', weights, value_states, precision=lax.Precision.HIGHEST)
    mixture = lax.map(jax.checkpoint(attend), jnp.arange(length // BLOCK, dtype=jnp.int32))
    mixture = jnp.moveaxis(mixture, 0, 1).reshape(packed, length, features)
    mixture = low(low_back(mixture))
    hidden = inputs + low_back(matmul(mixture, out_weight)) + out_bias
    normed_two = low(layer_norm(hidden, ln2_gain, ln2_bias))
    pre_active = low_back(matmul(normed_two, fc_weight)) + hidden_unit_bias
    activation_values = low(jax.nn.gelu(pre_active, approximate=True))
    return hidden + matmul(activation_values, proj_weight) + proj_bias

def reference(tokens, ln1_gain, ln1_bias, qkv_weight, qv_bias, out_weight, out_bias, ln2_gain, ln2_bias, fc_weight, hidden_unit_bias, proj_weight, proj_bias, cotangent):
    params = tuple((member.astype(jnp.float32) for member in (ln1_gain, ln1_bias, qkv_weight, qv_bias, out_weight, out_bias, ln2_gain, ln2_bias, fc_weight, hidden_unit_bias, proj_weight, proj_bias)))
    pack_size = math.gcd(SEQS, 4)
    inputs = tokens.astype(jnp.float32).reshape(SEQS // pack_size, pack_size, LEN, D)
    incoming = cotangent.astype(jnp.float32).reshape(SEQS // pack_size, pack_size, LEN, D)

    def advance(running, seq_group):
        group_in, group_grad = seq_group
        result, pullback = jax.vjp(forward, params, group_in)
        grad_params, grad_in = pullback(group_grad)
        running = jax.tree.map(jnp.add, running, grad_params)
        return (running, (result.astype(jnp.bfloat16), grad_in.astype(jnp.bfloat16)))
    empty_grads = jax.tree.map(jnp.zeros_like, params)
    totals, (outputs, grad_inputs) = lax.scan(advance, empty_grads, (inputs, incoming))
    return (outputs.reshape(SEQS, LEN, D), grad_inputs.reshape(SEQS, LEN, D), totals[0], totals[1], totals[2], totals[3], totals[4], totals[5], totals[6], totals[7], totals[8], totals[9], totals[10], totals[11])
```

```python
from functools import partial

import jax
import jax.numpy as jnp
from jax import lax
from jax.sharding import PartitionSpec as P

HEAD_DIM = 64
F32 = jnp.float32
LOW = jnp.bfloat16

CORE = [(i, i ^ 1) for i in range(16)]
PAIR = [(0, 1), (1, 0)]
SWAP = [
    ((q * 2 + c) * 2 + h, (q * 2 + h) * 2 + c)
    for q in range(8)
    for c in range(2)
    for h in range(2)
]


def x_shift(k):
    return [(i, (i + k) % 4) for i in range(4)]


def y_shift(k):
    return [(z * 8 + y * 2 + c, z * 8 + (y + k) % 4 * 2 + c) for z in range(2) for y in range(4) for c in range(2)]


Z_FLIP = [(i, i ^ 8) for i in range(16)]


def other_core(array):
    return lax.ppermute(array, "dp", CORE)


def swapped(array):
    return lax.ppermute(array, ("dp", "context"), SWAP)


def x_sent(array, k):
    return lax.ppermute(array, "tensor", x_shift(k))


def y_sent(array, k):
    return lax.ppermute(array, "dp", y_shift(k))


def in_order(parts, place):
    turned = [parts[0], parts[3], parts[2], parts[1]]
    twice = jnp.concatenate([p[None] for p in turned + turned[:3]], axis=0)
    return lax.dynamic_slice_in_dim(twice, (4 - place) % 4, 4, 0)


def two_in_order(own, other, first):
    return jnp.stack((jnp.where(first, own, other), jnp.where(first, other, own)))


def x_parts(array):
    far = x_sent(array, 2)
    right = x_sent(array, 1)
    left = x_sent(array, 3)
    return [array, right, far, left]


def pick(array, place):
    return lax.dynamic_index_in_dim(array, place, 0, keepdims=False)


def x_exchange(array, place):
    far = x_sent(pick(array, (place + 2) % 4), 2)
    right = x_sent(pick(array, (place + 1) % 4), 1)
    left = x_sent(pick(array, (place + 3) % 4), 3)
    return [pick(array, place), right, far, left]


def added(parts):
    total = parts[0].astype(F32)
    for part in parts[1:]:
        total = total + part.astype(F32)
    return total


def norm_forward(values_in, norm_gain, norm_bias):
    average = jnp.mean(values_in, axis=-1, keepdims=True)
    centred = values_in - average
    spread = jnp.mean(centred * centred, axis=-1, keepdims=True)
    factor = lax.rsqrt(spread + 1e-05)
    normal = centred * factor
    return (normal * norm_gain + norm_bias, normal, factor)


def norm_backward(grad_norm, normal, factor, norm_gain):
    grad_gain = jnp.sum(grad_norm * normal, axis=0)
    grad_shift = jnp.sum(grad_norm, axis=0)
    scaled = grad_norm * norm_gain
    first_term = jnp.mean(scaled, axis=-1, keepdims=True)
    second = jnp.mean(scaled * normal, axis=-1, keepdims=True)
    return (factor * (scaled - first_term - normal * second), grad_gain, grad_shift)


def gelu_back(pre_active, grad_active):
    unused, pullback = jax.vjp(partial(jax.nn.gelu, approximate=True), pre_active)
    return pullback(grad_active)[0]


def dot(left, right, dims):
    return lax.dot_general(left, right, (dims, ((), ())), preferred_element_type=F32)


def heads_of(array):
    return array.reshape(array.shape[0], 2, HEAD_DIM)


def scores_of(queries, keys):
    scores = jnp.einsum("qhd,khd->hqk", queries, keys, preferred_element_type=F32) * HEAD_DIM**-0.5
    length = queries.shape[0]
    visible = lax.iota(jnp.int32, length)[:, None] >= lax.iota(jnp.int32, length)[None, :]
    return jnp.where(visible[None], scores, -1e30)


def attend_forward(queries, keys, values):
    scores = scores_of(queries, keys)
    largest = jnp.max(scores, axis=-1, keepdims=True)
    powers = jnp.exp(scores - largest)
    summed = jnp.sum(powers, axis=-1, keepdims=True)
    weights = (powers / summed).astype(LOW)
    mixture = jnp.einsum("hqk,khd->qhd", weights, values, preferred_element_type=F32)
    return mixture.astype(LOW).reshape(queries.shape[0], 128), largest + jnp.log(summed)


def attend_backward(queries, keys, values, log_totals, grad):
    scores = scores_of(queries, keys)
    weights = jnp.exp(scores - log_totals)
    grad_values = jnp.einsum("hqk,qhd->khd", weights.astype(LOW), grad, preferred_element_type=F32)
    grad_weights = jnp.einsum("qhd,khd->hqk", grad, values, preferred_element_type=F32)
    grad_scores = weights * (grad_weights - jnp.sum(weights * grad_weights, axis=-1, keepdims=True))
    grad_low = grad_scores.astype(LOW)
    scaling = HEAD_DIM**-0.5
    grad_queries = jnp.einsum("hqk,khd->qhd", grad_low, keys, preferred_element_type=F32) * scaling
    grad_keys = jnp.einsum("hqk,qhd->khd", grad_low, queries, preferred_element_type=F32) * scaling
    return jnp.stack((grad_queries, grad_keys, grad_values), axis=1).astype(LOW).reshape(queries.shape[0], 3, 128)


def body(
    tokens,
    ln1_gain,
    ln1_bias,
    qkv_weight,
    qv_bias,
    out_weight,
    out_bias,
    ln2_gain,
    ln2_bias,
    fc_weight,
    hidden_unit_bias,
    proj_weight,
    proj_bias,
    cotangent,
):
    dp = lax.axis_index("dp")
    core, y, z_lo = dp % 2, dp // 2 % 4, dp // 8
    x = lax.axis_index("tensor")
    first_core = core == 0

    my_tokens = swapped(tokens[0])
    inputs = my_tokens.astype(F32)
    normed_one, normal_one, factor_one = norm_forward(inputs, ln1_gain, ln1_bias)
    normed_parts = x_parts(normed_one.astype(LOW))

    shard = jnp.concatenate((qkv_weight.transpose(1, 0, 2).reshape(64, 768), out_weight.T), axis=1)
    both = two_in_order(shard, lax.ppermute(shard, "dp", Z_FLIP), z_lo == 0)
    lines = in_order([both, y_sent(both, 1), y_sent(both, 2), y_sent(both, 3)], y)
    half = lines.transpose(1, 0, 2, 3).reshape(8, 64, 1024)
    other_half = other_core(half)
    weights_in = jnp.stack(
        (jnp.where(first_core, half, other_half), jnp.where(first_core, other_half, half)), axis=1
    ).reshape(1024, 1024)
    qkv_whole = weights_in[:, :768]
    out_share = lax.dynamic_slice_in_dim(weights_in, 768 + core * 128, 128, 1)
    out_lines = in_order(x_parts(out_share), x)
    out_other = other_core(out_lines)
    out_whole = two_in_order(out_lines, out_other, first_core)
    out_whole = out_whole.transpose(2, 1, 0, 3).reshape(1024, 1024)

    packed = jnp.concatenate((fc_weight, proj_weight.T), axis=0)
    packed = lax.all_gather(packed, "dp", axis=0)
    fc_whole = packed[:, :64].reshape(1024, 1024)
    proj_whole = packed[:, 64:].reshape(1024, 1024)

    cot_low = swapped(cotangent[0])
    cot_rows = jnp.concatenate(x_parts(cot_low), axis=0)
    grad_output = cot_low.astype(F32)

    normed_rows = in_order(normed_parts, x).reshape(512, 1024)
    shift = jnp.concatenate((qv_bias[0], jnp.zeros_like(qv_bias[0]), qv_bias[1]))
    qkv = (dot(normed_rows, qkv_whole, ((1,), (0,))) + shift).astype(LOW).reshape(512, 3, 2, 128)
    qkv_mine = jnp.where(first_core, qkv[:, :, 0], qkv[:, :, 1])
    qkv_gone = jnp.where(first_core, qkv[:, :, 1], qkv[:, :, 0])
    qkv_all = two_in_order(qkv_mine, other_core(qkv_gone), first_core).reshape(1024, 3, 128)
    queries, keys, values = heads_of(qkv_all[:, 0]), heads_of(qkv_all[:, 1]), heads_of(qkv_all[:, 2])
    mixture_heads, log_totals = attend_forward(queries, keys, values)

    halves = mixture_heads.reshape(2, 512, 128)
    mix_mine = jnp.where(first_core, halves[0], halves[1])
    mix_gone = jnp.where(first_core, halves[1], halves[0])
    mix_got = other_core(mix_gone)
    mixture_rows = jnp.concatenate(
        (jnp.where(first_core, mix_mine, mix_got), jnp.where(first_core, mix_got, mix_mine)), axis=1
    )
    mixture_parts = in_order(x_exchange(mixture_rows.reshape(4, 128, 256), x), x)
    mixture = mixture_parts.transpose(1, 0, 2).reshape(128, 1024)

    hidden = inputs + dot(mixture, out_whole, ((1,), (1,))) + out_bias
    normed_two, normal_two, factor_two = norm_forward(hidden, ln2_gain, ln2_bias)
    two_rows = jnp.concatenate(x_parts(normed_two.astype(LOW)), axis=0)

    pre_active = dot(two_rows, fc_whole, ((1,), (0,))) + hidden_unit_bias
    active = jax.nn.gelu(pre_active, approximate=True).astype(LOW)
    grad_active = dot(cot_rows, proj_whole, ((1,), (0,)))
    grad_pre = gelu_back(pre_active, grad_active)
    grad_pre_low = grad_pre.astype(LOW)
    back_terms = dot(grad_pre_low, fc_whole, ((1,), (1,))).astype(LOW).reshape(4, 128, 1024)
    back_two = added([back_terms[0]] + [x_sent(back_terms[k], -k) for k in (2, 1, 3)])
    grad_norm_two, grad_ln2_gain, grad_ln2_shift = norm_backward(back_two, normal_two, factor_two, ln2_gain)
    grad_hidden = grad_output + grad_norm_two
    hidden_low = grad_hidden.astype(LOW)

    grad_mixture = dot(hidden_low, out_whole, ((1,), (0,))).astype(LOW)
    grad_mix_parts = grad_mixture.reshape(128, 4, 256).transpose(1, 0, 2)
    grad_mix_rows = in_order(x_exchange(grad_mix_parts, x), x).reshape(512, 256)
    gm_mine = jnp.where(first_core, grad_mix_rows[:, :128], grad_mix_rows[:, 128:])
    gm_gone = jnp.where(first_core, grad_mix_rows[:, 128:], grad_mix_rows[:, :128])
    grad_mix_heads = two_in_order(gm_mine, other_core(gm_gone), first_core).reshape(1024, 2, HEAD_DIM)

    grad_qkv = attend_backward(queries, keys, values, log_totals, grad_mix_heads)

    grad_halves = grad_qkv.reshape(2, 512, 3, 128)
    gq_mine = jnp.where(first_core, grad_halves[0], grad_halves[1])
    gq_gone = jnp.where(first_core, grad_halves[1], grad_halves[0])
    gq_got = other_core(gq_gone)
    gq_rows = jnp.stack(
        (jnp.where(first_core, gq_mine, gq_got), jnp.where(first_core, gq_got, gq_mine)), axis=2
    ).reshape(512, 768)
    one_terms = dot(gq_rows, qkv_whole, ((1,), (1,))).astype(LOW).reshape(4, 128, 1024)
    back_one = added(x_exchange(one_terms, x))
    grad_norm_one, grad_ln1_gain, grad_ln1_shift = norm_backward(back_one, normal_one, factor_one, ln1_gain)
    grad_tokens = swapped((grad_hidden + grad_norm_one).astype(LOW))[None]

    out_terms = dot(active, proj_whole, ((1,), (1,))).astype(LOW).reshape(4, 128, 1024)
    mlp_sum = added([out_terms[0]] + [x_sent(out_terms[k], -k) for k in (2, 1, 3)])
    output = swapped((hidden + mlp_sum + proj_bias).astype(LOW))[None]

    grad_fc_w = dot(two_rows, grad_pre_low, ((0,), (0,))).astype(LOW)
    grad_proj_w = dot(cot_rows, active, ((0,), (0,))).astype(LOW)
    wide = jnp.concatenate((grad_fc_w.reshape(16, 64, 1024), grad_proj_w.reshape(16, 64, 1024)), axis=1)
    wide = lax.psum_scatter(wide, "dp", scatter_dimension=0, tiled=False)
    wide = wide.astype(F32) + lax.ppermute(wide, "context", PAIR).astype(F32)
    fc_total, proj_total = wide[:64], wide[64:].T

    hidden_rows = in_order(x_parts(hidden_low), x).reshape(512, 1024)
    grad_out_w = dot(hidden_rows, mixture_rows, ((0,), (0,))).astype(LOW)
    grad_out_w = grad_out_w.reshape(2, 4, 2, 64, 256)
    go_mine = jnp.where(first_core, grad_out_w[:, :, 0], grad_out_w[:, :, 1])
    go_gone = jnp.where(first_core, grad_out_w[:, :, 1], grad_out_w[:, :, 0])
    go_sum = (go_mine.astype(F32) + other_core(go_gone).astype(F32)).astype(LOW)
    go_sum = go_sum.reshape(2, 4, 128, 128)

    normed_other = other_core(normed_rows)
    normed_all = two_in_order(normed_rows, normed_other, first_core).reshape(1024, 1024)
    grad_qkv_w = dot(normed_all, grad_qkv.reshape(1024, 384), ((0,), (0,))).astype(LOW)
    grad_qkv_w = grad_qkv_w.reshape(2, 4, 128, 3, 128)
    gw = jnp.concatenate((go_sum, grad_qkv_w.transpose(0, 1, 3, 2, 4).reshape(2, 4, 384, 128)), axis=2)
    gw = gw.transpose(1, 0, 2, 3)
    got = [pick(gw, y)] + [y_sent(pick(gw, (y + k) % 4), k) for k in (2, 1, 3)]
    gw = added(got).astype(LOW)
    gw_keep, gw_go = pick(gw, z_lo), pick(gw, 1 - z_lo)
    gw_sum = (gw_keep.astype(F32) + lax.ppermute(gw_go, "dp", Z_FLIP).astype(F32)).astype(LOW)
    gw_sum = gw_sum.astype(F32) + lax.ppermute(gw_sum, "context", PAIR).astype(F32)
    out_total = gw_sum[:128].reshape(64, 256).T
    qkv_sum = gw_sum[128:].reshape(3, 2, 64, 128).astype(LOW)
    qk_mine = pick(qkv_sum.transpose(1, 0, 2, 3), core)
    qk_gone = pick(qkv_sum.transpose(1, 0, 2, 3), 1 - core)
    qk_got = other_core(qk_gone)
    qkv_total = jnp.concatenate(
        (jnp.where(first_core, qk_mine, qk_got), jnp.where(first_core, qk_got, qk_mine)), axis=-1
    ).astype(F32)

    grad_fc_shift = jnp.sum(grad_pre, axis=0)
    qv_sums = jnp.sum(grad_qkv.astype(F32), axis=0)
    qv_sums = jnp.stack((qv_sums[0], qv_sums[2]))
    low_half = jnp.where(first_core, qv_sums, 0.0)
    high_half = jnp.where(first_core, 0.0, qv_sums)
    qv_flat = jnp.concatenate((low_half, high_half), axis=1).reshape(512)
    whole = jnp.stack(
        (
            grad_ln1_gain,
            grad_ln1_shift,
            grad_ln2_gain,
            grad_ln2_shift,
            jnp.sum(grad_hidden, axis=0),
            jnp.sum(grad_output, axis=0),
        )
    )
    whole = added([whole] + [x_sent(whole, k) for k in (1, 2, 3)])
    vectors = jnp.concatenate((whole.reshape(6144), grad_fc_shift, qv_flat)).reshape(60, 128)
    vectors = vectors + other_core(vectors)
    vectors = added([vectors] + [y_sent(vectors, k) for k in (1, 2, 3)])
    vectors = vectors + lax.ppermute(vectors, "dp", Z_FLIP)
    vectors = vectors + lax.ppermute(vectors, "context", PAIR)
    vectors = vectors.reshape(7680)
    total = vectors[:6144].reshape(6, 1024)
    fc_shift_total = vectors[6144:7168]
    qv_total = vectors[7168:].reshape(2, 256)

    return (
        output,
        grad_tokens,
        total[0],
        total[1],
        qkv_total,
        qv_total,
        out_total,
        total[4],
        total[2],
        total[3],
        fc_total,
        fc_shift_total,
        proj_total,
        total[5],
    )


def solution(mesh):
    in_specs = (
        P("dp", ("context", "tensor"), None),
        P(),
        P(),
        P(None, "dp", "tensor"),
        P(None, "tensor"),
        P("tensor", "dp"),
        P(),
        P(),
        P(),
        P("dp", "tensor"),
        P("tensor"),
        P("tensor", "dp"),
        P(),
        P("dp", ("context", "tensor"), None),
    )
    out_specs = (
        P("dp", ("context", "tensor"), None),
        P("dp", ("context", "tensor"), None),
        P(),
        P(),
        P(None, "dp", "tensor"),
        P(None, "tensor"),
        P("tensor", "dp"),
        P(),
        P(),
        P(),
        P("dp", "tensor"),
        P("tensor"),
        P("tensor", "dp"),
        P(),
    )
    return jax.shard_map(body, mesh=mesh, in_specs=in_specs, out_specs=out_specs, check_vma=False)
```

```python
from functools import partial

import jax
import jax.numpy as jnp
from jax import lax
from jax.experimental import pallas as pl
from jax.experimental.pallas import tpu as pltpu
from jax.experimental import pallas as pl
from jax.experimental.pallas import tpu as pltpu
from jax.experimental import pallas as pl
from jax.experimental.pallas import tpu as pltpu
from jax.experimental import pallas as pl
from jax.experimental.pallas import tpu as pltpu
from jax.experimental import pallas as pl
from jax.experimental.pallas import tpu as pltpu
from jax.experimental import pallas as pl
from jax.experimental.pallas import tpu as pltpu
from jax.experimental import pallas as pl
from jax.experimental.pallas import tpu as pltpu
from jax.experimental import pallas as pl
from jax.experimental.pallas import tpu as pltpu
from jax.experimental import pallas as pl
from jax.experimental.pallas import tpu as pltpu
from jax.experimental import pallas as pl
from jax.experimental.pallas import tpu as pltpu
from jax.experimental import pallas as pl
from jax.experimental.pallas import tpu as pltpu
from jax.experimental import pallas as pl
from jax.experimental.pallas import tpu as pltpu
from jax.experimental import pallas as pl
from jax.experimental.pallas import tpu as pltpu
from jax.experimental import pallas as pl
from jax.experimental.pallas import tpu as pltpu
from jax.sharding import PartitionSpec as P

HEAD_DIM = 64
F32 = jnp.float32
LOW = jnp.bfloat16

CORE = [(i, i ^ 1) for i in range(16)]
PAIR = [(0, 1), (1, 0)]
SAME_CORE = [[i + core for i in range(0, 16, 2)] for core in range(2)]
ROWS = 512
TILE = 256


def x_shift(k):
    return [(i, (i + k) % 4) for i in range(4)]


def swap_shift(k):
    pairs = []
    for q in range(8):
        for c in range(2):
            for h in range(2):
                for x in range(4):
                    pairs.append((((q * 2 + c) * 2 + h) * 4 + x, ((q * 2 + h) * 2 + c) * 4 + (x + k) % 4))
    return pairs


def swapped(array, k=0):
    return lax.ppermute(array, ("dp", "context", "tensor"), swap_shift(k))


def other_core(array):
    return lax.ppermute(array, "dp", CORE)


def x_sent(array, k):
    return lax.ppermute(array, "tensor", x_shift(k))


def x_parts(array):
    far = x_sent(array, 2)
    right = x_sent(array, 1)
    left = x_sent(array, 3)
    return [array, right, far, left]


def x_back(parts):
    far = x_sent(parts[2], 2)
    right = x_sent(parts[1], 3)
    left = x_sent(parts[3], 1)
    return [parts[0], right, far, left]


def pick(array, place, dim=0):
    return lax.dynamic_index_in_dim(array, place, dim, keepdims=False)


def added(parts):
    total = parts[0].astype(F32)
    for part in parts[1:]:
        total = total + part.astype(F32)
    return total


def summed_over_dp(array):
    return lax.psum_scatter(array, "dp", scatter_dimension=0, axis_index_groups=SAME_CORE, tiled=True)


def norm_forward(values_in, norm_gain, norm_bias):
    average = jnp.mean(values_in, axis=-1, keepdims=True)
    centred = values_in - average
    spread = jnp.mean(centred * centred, axis=-1, keepdims=True)
    factor = lax.rsqrt(spread + 1e-05)
    normal = centred * factor
    return (normal * norm_gain + norm_bias, normal, factor)


def norm_backward(grad_norm, normal, factor, norm_gain):
    scaled = grad_norm * norm_gain
    first_term = jnp.mean(scaled, axis=-1, keepdims=True)
    second = jnp.mean(scaled * normal, axis=-1, keepdims=True)
    return factor * (scaled - first_term - normal * second)


def gelu_and_slope(values_in):
    root = (2.0 / jnp.pi) ** 0.5
    squared = values_in * values_in
    bent = jnp.tanh(root * values_in * (1.0 + 0.044715 * squared))
    part = 0.5 * (1.0 + bent)
    slope = part + 0.5 * values_in * (1.0 - bent * bent) * root * (1.0 + 3.0 * 0.044715 * squared)
    return values_in * part, slope


def together(*arrays):
    return lax.optimization_barrier(arrays)


def dot(left, right, left_dim=1, right_dim=0):
    return lax.dot_general(left, right, (((left_dim,), (right_dim,)), ((), ())), preferred_element_type=F32)


def exact_dot(left, right):
    return lax.dot_general(left, right, (((1,), (1,)), ((), ())), precision=lax.Precision.HIGHEST, preferred_element_type=F32)


def column_sums(array):
    return dot(jnp.ones((1, array.shape[0]), array.dtype), array)


def place_of(ids, chunk):
    return (chunk // 4 ^ ids[0]) * 4 + lax.rem(ids[1] + 4 - chunk % 4, 4)


def head_lanes(rows, head):
    lanes = lax.broadcasted_iota(jnp.int32, (rows, 2 * HEAD_DIM), 1)
    return lanes < HEAD_DIM if head == 0 else lanes >= HEAD_DIM


def collect(ids, qkv, queries, keys, values):
    for chunk in range(8):
        rows = slice(chunk * 128, chunk * 128 + 128)
        place = place_of(ids, chunk)
        queries[rows] = qkv[place, :, 0:128] * jnp.asarray(HEAD_DIM**-0.5, LOW)
        keys[rows] = qkv[place, :, 128:256]
        values[rows] = qkv[place, :, 256:384]


def visible_tile():
    key_place = lax.broadcasted_iota(jnp.int32, (TILE, TILE), 0)
    return key_place <= lax.broadcasted_iota(jnp.int32, (TILE, TILE), 1)


def forward_kernel(ids, qkv, mixture, totals, queries, keys, values, mixed):
    collect(ids, qkv, queries, keys, values)
    turned = values[...].T
    for block in range(1024 // TILE):
        rows = slice(block * TILE, block * TILE + TILE)
        before = block * TILE
        kept = []
        for head in range(2):
            row_block = jnp.where(head_lanes(TILE, head), queries[rows], jnp.zeros((), LOW))
            edge = dot(keys[rows], row_block, 1, 1)
            edge = jnp.where(visible_tile(), edge, -1e30)
            largest = jnp.max(edge, axis=0, keepdims=True)
            if before:
                early = dot(keys[:before], row_block, 1, 1)
                largest = jnp.maximum(largest, jnp.max(early, axis=0, keepdims=True))
            powers = jnp.exp(edge - largest)
            summed = jnp.sum(powers, axis=0, keepdims=True)
            mix = dot(turned[:, rows], powers.astype(LOW))
            if before:
                powers = jnp.exp(early - largest)
                summed = summed + jnp.sum(powers, axis=0, keepdims=True)
                mix = mix + dot(turned[:, :before], powers.astype(LOW))
            kept.append(mix / summed)
            totals[head : head + 1, rows] = largest + jnp.log(summed)
        features = lax.broadcasted_iota(jnp.int32, (128, TILE), 0)
        mixed[rows] = jnp.where(features < HEAD_DIM, kept[0], kept[1]).T.astype(LOW)
    for chunk in range(8):
        mixture[place_of(ids, chunk)] = mixed[chunk * 128 : chunk * 128 + 128]


def backward_kernel(
    ids, qkv, totals, grad, grad_qkv, queries, keys, values, grads, grad_queries, grad_keys, grad_values
):
    collect(ids, qkv, queries, keys, values)
    for chunk in range(8):
        grads[chunk * 128 : chunk * 128 + 128] = grad[place_of(ids, chunk)]
    turned = keys[...].T
    for block in reversed(range(1024 // TILE)):
        rows = slice(block * TILE, block * TILE + TILE)
        before = block * TILE
        pieces = [rows, slice(0, before)] if before else [rows]
        sent = []
        for head in range(2):
            lanes = head_lanes(TILE, head)
            row_block = jnp.where(lanes, queries[rows], jnp.zeros((), LOW))
            grad_block = jnp.where(lanes, grads[rows], jnp.zeros((), LOW))
            total = totals[head : head + 1, rows]
            weights, products = [], []
            balance = jnp.zeros((1, TILE), F32)
            for piece in pieces:
                scores = dot(keys[piece], row_block, 1, 1)
                if piece is rows:
                    scores = jnp.where(visible_tile(), scores, -1e30)
                weight = jnp.exp(scores - total)
                product = dot(values[piece], grad_block, 1, 1)
                balance = balance + jnp.sum(weight * product, axis=0, keepdims=True)
                weights.append(weight)
                products.append(product)
            turned_grad = jnp.zeros((128, TILE), F32)
            for piece, weight, product in zip(pieces, weights, products):
                low = (weight * (product - balance)).astype(LOW)
                value_part = dot(weight.astype(LOW), grad_block)
                key_part = dot(low, row_block)
                if block == 1024 // TILE - 1 and head == 0:
                    grad_values[piece] = value_part
                    grad_keys[piece] = key_part
                else:
                    grad_values[piece] += value_part
                    grad_keys[piece] += key_part
                turned_grad = turned_grad + dot(turned[:, piece], low)
            sent.append(turned_grad)
        features = lax.broadcasted_iota(jnp.int32, (128, TILE), 0)
        grad_queries[rows] = jnp.where(features < HEAD_DIM, sent[0], sent[1]).T * HEAD_DIM**-0.5
    for chunk in range(8):
        rows = slice(chunk * 128, chunk * 128 + 128)
        place = place_of(ids, chunk)
        grad_qkv[place, :, 0:128] = grad_queries[rows].astype(LOW)
        grad_qkv[place, :, 128:256] = grad_keys[rows].astype(LOW)
        grad_qkv[place, :, 256:384] = grad_values[rows].astype(LOW)


SMEM = pl.BlockSpec(memory_space=pltpu.SMEM)
VMEM = pl.BlockSpec(memory_space=pltpu.VMEM)


def attend_forward(ids, qkv):
    return pl.pallas_call(
        forward_kernel,
        out_shape=(jax.ShapeDtypeStruct((8, 128, 128), LOW), jax.ShapeDtypeStruct((2, 1024), F32)),
        in_specs=[SMEM, VMEM],
        out_specs=(VMEM, VMEM),
        scratch_shapes=[pltpu.VMEM((1024, 128), LOW) for _ in range(4)],
        compiler_params=pltpu.CompilerParams(vmem_limit_bytes=24 * 2**20),
        cost_estimate=pl.CostEstimate(flops=700 * 2**20, bytes_accessed=2 * 2**20, transcendentals=2**20),
        name="attend_forward",
    )(ids, qkv)


def attend_backward(ids, qkv, totals, grad):
    return pl.pallas_call(
        backward_kernel,
        out_shape=jax.ShapeDtypeStruct((8, 128, 384), LOW),
        in_specs=[SMEM, VMEM, VMEM, VMEM],
        out_specs=VMEM,
        scratch_shapes=[pltpu.VMEM((1024, 128), LOW) for _ in range(4)]
        + [pltpu.VMEM((1024, 128), F32) for _ in range(3)],
        compiler_params=pltpu.CompilerParams(vmem_limit_bytes=32 * 2**20),
        cost_estimate=pl.CostEstimate(flops=1800 * 2**20, bytes_accessed=3 * 2**20, transcendentals=2**20),
        name="attend_backward",
    )(ids, qkv, totals, grad)


def body(
    tokens,
    ln1_gain,
    ln1_bias,
    qkv_weight,
    qv_bias,
    out_weight,
    out_bias,
    ln2_gain,
    ln2_bias,
    fc_weight,
    hidden_unit_bias,
    proj_weight,
    proj_bias,
    cotangent,
):
    dp = lax.axis_index("dp")
    core = dp % 2
    x = lax.axis_index("tensor")
    first_core = core == 0
    ids = jnp.stack((core, x)).astype(jnp.int32)

    pair = swapped(jnp.concatenate((tokens[0], cotangent[0]), axis=0))
    pairs = x_parts(pair)

    shard = qkv_weight.reshape(3, 64, 2, 128).transpose(1, 2, 0, 3).reshape(64, 768)
    line = lax.all_gather(jnp.concatenate((shard, out_weight.T, fc_weight), axis=1), "dp", axis=0, tiled=True)

    token_rows = jnp.concatenate([part[:128] for part in pairs], axis=0)
    cot_rows = jnp.concatenate([part[128:] for part in pairs], axis=0)
    grad_output = pair[128:].astype(F32)
    inputs = token_rows.astype(F32)
    normed_one, normal_one, factor_one = norm_forward(inputs, ln1_gain, ln1_bias)
    normed_rows, proj_shard = together(normed_one.astype(LOW), proj_weight.T)
    proj_shard, line = together(proj_shard, line)
    proj_whole = lax.all_gather(proj_shard, "dp", axis=0, tiled=True)
    normed_other = other_core(normed_rows)

    fc_whole = line[:, 1024:]
    qkv_own = lax.dynamic_slice_in_dim(line, core * 384, 384, 1)
    qkv_other = lax.dynamic_slice_in_dim(line, 384 - core * 384, 384, 1)
    out_own = lax.dynamic_slice_in_dim(line, 768 + core * 128, 128, 1)
    out_other = lax.dynamic_slice_in_dim(line, 896 - core * 128, 128, 1)

    shift = jnp.where(first_core, qv_bias[:, :128], qv_bias[:, 128:])
    shift = jnp.concatenate((shift[0], jnp.zeros_like(shift[0]), shift[1]))
    qkv = jnp.concatenate(
        ((dot(normed_rows, qkv_own) + shift).astype(LOW), (dot(normed_other, qkv_own) + shift).astype(LOW)), axis=0
    ).reshape(8, 128, 384)
    out_parts = x_parts(out_own)
    mixture_heads, log_totals = attend_forward(ids, qkv)
    mixture_heads, out_parts[1], out_parts[3] = together(mixture_heads, out_parts[1], out_parts[3])
    mixture_heads = mixture_heads.reshape(2, ROWS, 128)
    mixture_rows = jnp.concatenate((mixture_heads[0], other_core(mixture_heads[1])), axis=1)
    mixture_parts = x_parts(mixture_rows)

    out_others = [out_other] + [other_core(part) for part in out_parts[1:]]
    out_whole = jnp.concatenate([part for both in zip(out_parts, out_others) for part in both], axis=1)
    mixture = jnp.concatenate([jnp.roll(mixture_parts[k], 128 * k, 0) for k in range(4)], axis=1)
    hidden = inputs + dot(mixture, out_whole, 1, 1) + out_bias
    normed_two, normal_two, factor_two = norm_forward(hidden, ln2_gain, ln2_bias)
    two_rows = normed_two.astype(LOW)

    pre_active = dot(two_rows, fc_whole) + hidden_unit_bias
    active, slope = gelu_and_slope(pre_active)
    active, slope = together(active.astype(LOW), slope)
    grad_active = dot(cot_rows, proj_whole)
    grad_pre = slope * grad_active
    grad_pre_low = grad_pre.astype(LOW)
    back_terms = dot(grad_pre_low, fc_whole, 1, 1).astype(LOW)

    back_parts = x_back(back_terms.reshape(4, 128, 1024))
    back_two = added(back_parts)
    grad_fc_w = dot(two_rows, grad_pre_low, 0, 0).astype(LOW).reshape(2, 4, 2, 64, 1024)
    grad_proj_w = dot(cot_rows, active, 0, 0).astype(LOW).reshape(2, 4, 2, 64, 1024)
    fc_got = other_core(pick(grad_fc_w, 1 - core, 2))
    proj_got = other_core(pick(grad_proj_w, 1 - core, 2))
    wide = jnp.concatenate(
        (added([pick(grad_fc_w, core, 2), fc_got]), added([pick(grad_proj_w, core, 2), proj_got])), axis=2
    ).astype(LOW)
    back_two, wide = together(back_two, wide)
    wide = summed_over_dp(wide.reshape(1024, 1024))
    out_terms = dot(active, proj_whole, 1, 1).astype(LOW)

    normal_own, factor_own = normal_two[:128], factor_two[:128]
    grad_ln2_gain = jnp.sum(back_two * normal_own, axis=0)
    grad_ln2_shift = jnp.sum(back_two, axis=0)
    grad_hidden = grad_output + norm_backward(back_two, normal_own, factor_own, ln2_gain)

    extra = jnp.concatenate((jnp.stack((grad_ln2_gain, grad_ln2_shift)), jnp.zeros((14, 1024), F32)))
    carried = x_parts(jnp.concatenate((grad_hidden, extra)).astype(LOW))
    hidden_rows = jnp.concatenate([part[:128] for part in carried], axis=0)
    hidden_rows, out_terms = together(hidden_rows, out_terms)
    ln2_sums = added([part[128:130] for part in carried])

    grad_mixture = dot(hidden_rows, out_whole[:, :256]).astype(LOW)
    grad_heads = jnp.stack((grad_mixture[:, :128], other_core(grad_mixture[:, 128:])))
    grad_out_w = dot(hidden_rows, mixture_rows, 0, 0).astype(LOW)
    grad_out_w = grad_out_w.reshape(2, 4, 2, 64, 256)
    out_mine, out_gone = pick(grad_out_w, core, 2), pick(grad_out_w, 1 - core, 2)
    out_got = other_core(out_gone)
    out_sum = jnp.concatenate(
        (added([out_mine[..., :128], out_got[..., 128:]]), added([out_mine[..., 128:], out_got[..., :128]])), axis=2
    ).astype(LOW)

    vectors = jnp.concatenate((ln2_sums, column_sums(hidden_rows), column_sums(cot_rows), jnp.sum(grad_pre, axis=0)[None]))
    vectors = jnp.concatenate((vectors[:, :512], vectors[:, 512:])).astype(LOW)

    grad_heads, out_sum, vectors = together(grad_heads, out_sum, vectors)
    grad_qkv = attend_backward(ids, qkv, log_totals, grad_heads.reshape(8, 128, 128))
    grad_halves = grad_qkv.reshape(2, ROWS, 384)
    gq_got = other_core(grad_halves[1])

    grad_qkv_w = dot(normed_rows, grad_halves[0], 0, 0) + dot(normed_other, grad_halves[1], 0, 0)
    gq_sums = column_sums(grad_qkv.reshape(1024, 384))
    gq_high = gq_sums.astype(LOW)
    gq_rest = (gq_sums - gq_high.astype(F32)).astype(LOW)
    grad_ln1_shift = dot(jnp.concatenate((gq_high, gq_rest)), qkv_own, 1, 1).sum(axis=0, keepdims=True)
    terms = (qkv_own.astype(F32) * grad_qkv_w).astype(LOW)
    grad_ln1_gain = (dot(jnp.ones((1, 384), LOW), terms, 1, 1) - ln1_bias * grad_ln1_shift) / ln1_gain
    ln1_sums = jnp.concatenate((grad_ln1_gain, grad_ln1_shift))
    ln1_sums, gq_got = together(ln1_sums, gq_got)
    ln1_parts = [ln1_sums] + [x_sent(ln1_sums, k) for k in (2, 1, 3)]
    back_one = (dot(grad_halves[0], qkv_own, 1, 1) + dot(gq_got, qkv_other, 1, 1)).astype(LOW)
    back_one = jnp.concatenate((back_one.reshape(4, 128, 1024), out_terms.reshape(4, 128, 1024)), axis=1)
    back_one = x_back(back_one)
    ln1_sums = added(ln1_parts)
    qv_sums = jnp.concatenate((gq_sums[:, :128], gq_sums[:, 256:]), axis=1)
    qv_sums = jnp.concatenate((jnp.where(first_core, qv_sums, 0.0), jnp.where(first_core, 0.0, qv_sums)), axis=1)
    late = jnp.concatenate((ln1_sums[:, :512], ln1_sums[:, 512:], qv_sums, jnp.zeros((1, 512), F32))).astype(LOW)
    vectors = jnp.concatenate((late, vectors))

    both = jnp.concatenate((out_sum, grad_qkv_w.astype(LOW).reshape(2, 4, 128, 384)), axis=3)
    both = jnp.concatenate((both, jnp.broadcast_to(vectors, (2, 4, 16, 512))), axis=2)
    both, wide = together(both, wide)
    both = summed_over_dp(both.reshape(1152, 512))
    both = added([both, lax.ppermute(both, "context", PAIR)])
    back_one = added(back_one)
    grad_norm_one = norm_backward(back_one[:128], normal_one[:128], factor_one[:128], ln1_gain)
    results = jnp.concatenate((hidden[:128] + back_one[128:] + proj_bias, grad_hidden + grad_norm_one), axis=0)
    results = swapped(results.astype(LOW))
    output, grad_tokens = results[:128][None], results[128:][None]
    wide = added([wide, lax.ppermute(wide, "context", PAIR)])
    fc_total, proj_total = wide[:64], wide[64:].T
    gone = jnp.concatenate((lax.dynamic_slice_in_dim(both, (1 - core) * 64, 64, 0), both[128:]), axis=0)
    got = other_core(gone)
    out_sum, vectors = both[:128, :128], both[128:] + got[64:]
    qkv_mine = lax.dynamic_slice_in_dim(both, core * 64, 64, 0)[:, 128:].reshape(64, 3, 128)
    qkv_got = got[:64, 128:].reshape(64, 3, 128)
    qkv_total = jnp.concatenate(
        (jnp.where(first_core, qkv_mine, qkv_got), jnp.where(first_core, qkv_got, qkv_mine)), axis=-1
    ).transpose(1, 0, 2)
    out_total = jnp.concatenate(
        (jnp.where(first_core, out_sum[:64], out_sum[64:]), jnp.where(first_core, out_sum[64:], out_sum[:64])), axis=1
    ).T
    ln1_sums, qv_total = jnp.concatenate((vectors[0:2], vectors[2:4]), axis=1), vectors[4]
    vectors = jnp.concatenate((vectors[6:11], vectors[11:16]), axis=1)

    return (
        output,
        grad_tokens,
        ln1_sums[0],
        ln1_sums[1],
        qkv_total,
        qv_total.reshape(2, 2, 128).transpose(1, 0, 2).reshape(2, 256),
        out_total,
        vectors[2],
        vectors[0],
        vectors[1],
        fc_total,
        vectors[4],
        proj_total,
        vectors[3],
    )


def solution(mesh):
    in_specs = (
        P("dp", ("context", "tensor"), None),
        P(),
        P(),
        P(None, "dp", "tensor"),
        P(None, "tensor"),
        P("tensor", "dp"),
        P(),
        P(),
        P(),
        P("dp", "tensor"),
        P("tensor"),
        P("tensor", "dp"),
        P(),
        P("dp", ("context", "tensor"), None),
    )
    out_specs = (
        P("dp", ("context", "tensor"), None),
        P("dp", ("context", "tensor"), None),
        P(),
        P(),
        P(None, "dp", "tensor"),
        P(None, "tensor"),
        P("tensor", "dp"),
        P(),
        P(),
        P(),
        P("dp", "tensor"),
        P("tensor"),
        P("tensor", "dp"),
        P(),
    )
    return jax.shard_map(body, mesh=mesh, in_specs=in_specs, out_specs=out_specs, check_vma=False)
```

```python
from functools import partial

import jax
import jax.numpy as jnp
from jax import lax
from jax.experimental import pallas as pl
from jax.experimental.pallas import tpu as pltpu
from jax.experimental import pallas as pl
from jax.experimental.pallas import tpu as pltpu
from jax.experimental import pallas as pl
from jax.experimental.pallas import tpu as pltpu
from jax.experimental import pallas as pl
from jax.experimental.pallas import tpu as pltpu
from jax.experimental import pallas as pl
from jax.experimental.pallas import tpu as pltpu
from jax.experimental import pallas as pl
from jax.experimental.pallas import tpu as pltpu
from jax.experimental import pallas as pl
from jax.experimental.pallas import tpu as pltpu
from jax.experimental import pallas as pl
from jax.experimental.pallas import tpu as pltpu
from jax.experimental import pallas as pl
from jax.experimental.pallas import tpu as pltpu
from jax.experimental import pallas as pl
from jax.experimental.pallas import tpu as pltpu
from jax.experimental import pallas as pl
from jax.experimental.pallas import tpu as pltpu
from jax.experimental import pallas as pl
from jax.experimental.pallas import tpu as pltpu
from jax.experimental import pallas as pl
from jax.experimental.pallas import tpu as pltpu
from jax.experimental import pallas as pl
from jax.experimental.pallas import tpu as pltpu
from jax.experimental import pallas as pl
from jax.experimental.pallas import tpu as pltpu
from jax.experimental import pallas as pl
from jax.experimental.pallas import tpu as pltpu
from jax.experimental import pallas as pl
from jax.experimental.pallas import tpu as pltpu
from jax.experimental import pallas as pl
from jax.experimental.pallas import tpu as pltpu
from jax.sharding import PartitionSpec as P

HEAD_DIM = 64
F32 = jnp.float32
LOW = jnp.bfloat16

CORE = [(i, i ^ 1) for i in range(16)]
PAIR = [(0, 1), (1, 0)]
SAME_CORE = [[i + core for i in range(0, 16, 2)] for core in range(2)]
ROWS = 512
TILE = 256


def x_shift(k):
    return [(i, (i + k) % 4) for i in range(4)]


def swap_shift(k):
    pairs = []
    for q in range(8):
        for c in range(2):
            for h in range(2):
                for x in range(4):
                    pairs.append((((q * 2 + c) * 2 + h) * 4 + x, ((q * 2 + h) * 2 + c) * 4 + (x + k) % 4))
    return pairs


def swapped(array, k=0):
    return lax.ppermute(array, ("dp", "context", "tensor"), swap_shift(k))


def other_core(array):
    return lax.ppermute(array, "dp", CORE)


def x_sent(array, k):
    return lax.ppermute(array, "tensor", x_shift(k))


def x_parts(array):
    far = x_sent(array, 2)
    right = x_sent(array, 1)
    left = x_sent(array, 3)
    return [array, right, far, left]


def x_back(parts):
    far = x_sent(parts[2], 2)
    right = x_sent(parts[1], 3)
    left = x_sent(parts[3], 1)
    return [parts[0], right, far, left]


def pick(array, place, dim=0):
    return lax.dynamic_index_in_dim(array, place, dim, keepdims=False)


def added(parts):
    total = parts[0].astype(F32)
    for part in parts[1:]:
        total = total + part.astype(F32)
    return total


def summed_over_dp(array):
    return lax.psum_scatter(array, "dp", scatter_dimension=0, axis_index_groups=SAME_CORE, tiled=True)


def norm_forward(values_in, norm_gain, norm_bias):
    average = jnp.mean(values_in, axis=-1, keepdims=True)
    centred = values_in - average
    spread = jnp.mean(centred * centred, axis=-1, keepdims=True)
    factor = lax.rsqrt(spread + 1e-05)
    normal = centred * factor
    return (normal * norm_gain + norm_bias, normal, factor)


def norm_backward(grad_norm, normal, factor, norm_gain):
    scaled = grad_norm * norm_gain
    first_term = jnp.mean(scaled, axis=-1, keepdims=True)
    second = jnp.mean(scaled * normal, axis=-1, keepdims=True)
    return factor * (scaled - first_term - normal * second)


def gelu_and_slope(values_in):
    root = (2.0 / jnp.pi) ** 0.5
    squared = values_in * values_in
    bent = jnp.tanh(root * values_in * (1.0 + 0.044715 * squared))
    part = 0.5 * (1.0 + bent)
    slope = part + 0.5 * values_in * (1.0 - bent * bent) * root * (1.0 + 3.0 * 0.044715 * squared)
    return values_in * part, slope


def together(*arrays):
    return lax.optimization_barrier(arrays)


def dot(left, right, left_dim=1, right_dim=0):
    return lax.dot_general(left, right, (((left_dim,), (right_dim,)), ((), ())), preferred_element_type=F32)


def exact_dot(left, right):
    return lax.dot_general(left, right, (((1,), (1,)), ((), ())), precision=lax.Precision.HIGHEST, preferred_element_type=F32)


def column_sums(array):
    return dot(jnp.ones((1, array.shape[0]), array.dtype), array)


def place_of(ids, chunk):
    return (chunk // 4 ^ ids[0]) * 4 + lax.rem(ids[1] + 4 - chunk % 4, 4)


def head_lanes(rows, head):
    lanes = lax.broadcasted_iota(jnp.int32, (rows, 2 * HEAD_DIM), 1)
    return lanes < HEAD_DIM if head == 0 else lanes >= HEAD_DIM


def collect(ids, qkv, queries, keys, values):
    for chunk in range(8):
        rows = slice(chunk * 128, chunk * 128 + 128)
        place = place_of(ids, chunk)
        queries[rows] = qkv[place, :, 0:128] * jnp.asarray(HEAD_DIM**-0.5, LOW)
        keys[rows] = qkv[place, :, 128:256]
        values[rows] = qkv[place, :, 256:384]


def visible_tile():
    key_place = lax.broadcasted_iota(jnp.int32, (TILE, TILE), 0)
    return key_place <= lax.broadcasted_iota(jnp.int32, (TILE, TILE), 1)


def forward_kernel(ids, qkv, mixture, totals, queries, keys, values, mixed):
    collect(ids, qkv, queries, keys, values)
    turned = values[...].T
    for block in range(1024 // TILE):
        rows = slice(block * TILE, block * TILE + TILE)
        before = block * TILE
        kept = []
        for head in range(2):
            row_block = jnp.where(head_lanes(TILE, head), queries[rows], jnp.zeros((), LOW))
            edge = dot(keys[rows], row_block, 1, 1)
            edge = jnp.where(visible_tile(), edge, -1e30)
            largest = jnp.max(edge, axis=0, keepdims=True)
            if before:
                early = dot(keys[:before], row_block, 1, 1)
                largest = jnp.maximum(largest, jnp.max(early, axis=0, keepdims=True))
            powers = jnp.exp(edge - largest)
            summed = jnp.sum(powers, axis=0, keepdims=True)
            mix = dot(turned[:, rows], powers.astype(LOW))
            if before:
                powers = jnp.exp(early - largest)
                summed = summed + jnp.sum(powers, axis=0, keepdims=True)
                mix = mix + dot(turned[:, :before], powers.astype(LOW))
            kept.append(mix / summed)
            totals[head : head + 1, rows] = largest + jnp.log(summed)
        features = lax.broadcasted_iota(jnp.int32, (128, TILE), 0)
        mixed[rows] = jnp.where(features < HEAD_DIM, kept[0], kept[1]).T.astype(LOW)
    for chunk in range(8):
        mixture[place_of(ids, chunk)] = mixed[chunk * 128 : chunk * 128 + 128]


def backward_kernel(
    ids, qkv, totals, grad, grad_qkv, queries, keys, values, grads, grad_queries, grad_keys, grad_values
):
    collect(ids, qkv, queries, keys, values)
    for chunk in range(8):
        grads[chunk * 128 : chunk * 128 + 128] = grad[place_of(ids, chunk)]
    turned = keys[...].T
    for block in reversed(range(1024 // TILE)):
        rows = slice(block * TILE, block * TILE + TILE)
        before = block * TILE
        pieces = [rows, slice(0, before)] if before else [rows]
        sent = []
        for head in range(2):
            lanes = head_lanes(TILE, head)
            row_block = jnp.where(lanes, queries[rows], jnp.zeros((), LOW))
            grad_block = jnp.where(lanes, grads[rows], jnp.zeros((), LOW))
            total = totals[head : head + 1, rows]
            weights, products = [], []
            balance = jnp.zeros((1, TILE), F32)
            for piece in pieces:
                scores = dot(keys[piece], row_block, 1, 1)
                if piece is rows:
                    scores = jnp.where(visible_tile(), scores, -1e30)
                weight = jnp.exp(scores - total)
                product = dot(values[piece], grad_block, 1, 1)
                balance = balance + jnp.sum(weight * product, axis=0, keepdims=True)
                weights.append(weight)
                products.append(product)
            turned_grad = jnp.zeros((128, TILE), F32)
            for piece, weight, product in zip(pieces, weights, products):
                low = (weight * (product - balance)).astype(LOW)
                value_part = dot(weight.astype(LOW), grad_block)
                key_part = dot(low, row_block)
                if block == 1024 // TILE - 1 and head == 0:
                    grad_values[piece] = value_part
                    grad_keys[piece] = key_part
                else:
                    grad_values[piece] += value_part
                    grad_keys[piece] += key_part
                turned_grad = turned_grad + dot(turned[:, piece], low)
            sent.append(turned_grad)
        features = lax.broadcasted_iota(jnp.int32, (128, TILE), 0)
        grad_queries[rows] = jnp.where(features < HEAD_DIM, sent[0], sent[1]).T * HEAD_DIM**-0.5
    for chunk in range(8):
        rows = slice(chunk * 128, chunk * 128 + 128)
        place = place_of(ids, chunk)
        grad_qkv[place, :, 0:128] = grad_queries[rows].astype(LOW)
        grad_qkv[place, :, 128:256] = grad_keys[rows].astype(LOW)
        grad_qkv[place, :, 256:384] = grad_values[rows].astype(LOW)


SMEM = pl.BlockSpec(memory_space=pltpu.SMEM)
VMEM = pl.BlockSpec(memory_space=pltpu.VMEM)


def attend_forward(ids, qkv):
    return pl.pallas_call(
        forward_kernel,
        out_shape=(jax.ShapeDtypeStruct((8, 128, 128), LOW), jax.ShapeDtypeStruct((2, 1024), F32)),
        in_specs=[SMEM, VMEM],
        out_specs=(VMEM, VMEM),
        scratch_shapes=[pltpu.VMEM((1024, 128), LOW) for _ in range(4)],
        compiler_params=pltpu.CompilerParams(vmem_limit_bytes=24 * 2**20),
        cost_estimate=pl.CostEstimate(flops=700 * 2**20, bytes_accessed=2 * 2**20, transcendentals=2**20),
        name="attend_forward",
    )(ids, qkv)


def attend_backward(ids, qkv, totals, grad):
    return pl.pallas_call(
        backward_kernel,
        out_shape=jax.ShapeDtypeStruct((8, 128, 384), LOW),
        in_specs=[SMEM, VMEM, VMEM, VMEM],
        out_specs=VMEM,
        scratch_shapes=[pltpu.VMEM((1024, 128), LOW) for _ in range(4)]
        + [pltpu.VMEM((1024, 128), F32) for _ in range(3)],
        compiler_params=pltpu.CompilerParams(vmem_limit_bytes=32 * 2**20),
        cost_estimate=pl.CostEstimate(flops=1800 * 2**20, bytes_accessed=3 * 2**20, transcendentals=2**20),
        name="attend_backward",
    )(ids, qkv, totals, grad)


def body(
    tokens,
    ln1_gain,
    ln1_bias,
    qkv_weight,
    qv_bias,
    out_weight,
    out_bias,
    ln2_gain,
    ln2_bias,
    fc_weight,
    hidden_unit_bias,
    proj_weight,
    proj_bias,
    cotangent,
):
    dp = lax.axis_index("dp")
    core = dp % 2
    x = lax.axis_index("tensor")
    first_core = core == 0
    ids = jnp.stack((core, x)).astype(jnp.int32)

    token_parts = x_parts(swapped(tokens[0]))
    cot_own = swapped(cotangent[0])
    cot_rows = jnp.concatenate(x_parts(cot_own), axis=0)

    shard = qkv_weight.reshape(3, 64, 2, 128).transpose(1, 2, 0, 3).reshape(64, 768)
    line = lax.all_gather(jnp.concatenate((shard, out_weight.T), axis=1), "dp", axis=0, tiled=True)

    token_rows = jnp.concatenate(token_parts, axis=0)
    inputs = token_rows.astype(F32)
    normed_one, normal_one, factor_one = norm_forward(inputs, ln1_gain, ln1_bias)
    shard = jnp.concatenate((fc_weight, proj_weight.T), axis=1)
    normed_rows, shard, cot_rows = together(normed_one.astype(LOW), shard, cot_rows)
    shard, line = together(shard, line)
    packed = lax.all_gather(shard, "dp", axis=0, tiled=True)
    fc_whole, proj_whole = packed[:, :1024], packed[:, 1024:]
    normed_other = other_core(normed_rows)
    grad_output = cot_own.astype(F32)

    qkv_own = lax.dynamic_slice_in_dim(line, core * 384, 384, 1)
    qkv_other = lax.dynamic_slice_in_dim(line, 384 - core * 384, 384, 1)
    out_own = lax.dynamic_slice_in_dim(line, 768 + core * 128, 128, 1)
    out_other = lax.dynamic_slice_in_dim(line, 896 - core * 128, 128, 1)

    shift = jnp.where(first_core, qv_bias[:, :128], qv_bias[:, 128:])
    shift = jnp.concatenate((shift[0], jnp.zeros_like(shift[0]), shift[1]))
    qkv = jnp.concatenate(
        ((dot(normed_rows, qkv_own) + shift).astype(LOW), (dot(normed_other, qkv_own) + shift).astype(LOW)), axis=0
    ).reshape(8, 128, 384)
    qkv, out_own = together(qkv, out_own)
    out_parts = x_parts(out_own)
    mixture_heads, log_totals = attend_forward(ids, qkv)
    mixture_heads = mixture_heads.reshape(2, ROWS, 128)
    mixture_rows = jnp.concatenate((mixture_heads[0], other_core(mixture_heads[1])), axis=1)
    mixture_parts = x_parts(mixture_rows)

    out_others = [out_other] + [other_core(part) for part in out_parts[1:]]
    out_whole = jnp.concatenate([part for both in zip(out_parts, out_others) for part in both], axis=1)
    mixture = jnp.concatenate([jnp.roll(mixture_parts[k], 128 * k, 0) for k in range(4)], axis=1)
    hidden = inputs + dot(mixture, out_whole, 1, 1) + out_bias
    normed_two, normal_two, factor_two = norm_forward(hidden, ln2_gain, ln2_bias)
    two_rows = normed_two.astype(LOW)

    pre_active = dot(two_rows, fc_whole) + hidden_unit_bias
    active, slope = gelu_and_slope(pre_active)
    active, slope = together(active.astype(LOW), slope)
    grad_active = dot(cot_rows, proj_whole)
    grad_pre = slope * grad_active
    grad_pre_low = grad_pre.astype(LOW)
    back_terms = dot(grad_pre_low, fc_whole, 1, 1).astype(LOW)

    back_parts = x_back(back_terms.reshape(4, 128, 1024))
    back_two = added(back_parts)
    grad_fc_w = dot(two_rows, grad_pre_low, 0, 0).astype(LOW).reshape(2, 4, 2, 64, 1024)
    grad_proj_w = dot(cot_rows, active, 0, 0).astype(LOW).reshape(2, 4, 2, 64, 1024)
    gone = jnp.concatenate((pick(grad_fc_w, 1 - core, 2), pick(grad_proj_w, 1 - core, 2)), axis=2)
    mine = jnp.concatenate((pick(grad_fc_w, core, 2), pick(grad_proj_w, core, 2)), axis=2)
    wide = added([mine, other_core(gone)]).astype(LOW)
    back_two, wide = together(back_two, wide)
    wide = summed_over_dp(wide.reshape(1024, 1024))
    out_terms = dot(active, proj_whole, 1, 1).astype(LOW)

    normal_own, factor_own = normal_two[:128], factor_two[:128]
    grad_ln2_gain = jnp.sum(back_two * normal_own, axis=0, keepdims=True)
    grad_ln2_shift = jnp.sum(back_two, axis=0, keepdims=True)
    grad_hidden = grad_output + norm_backward(back_two, normal_own, factor_own, ln2_gain)

    hidden_rows = jnp.concatenate(x_parts(grad_hidden.astype(LOW)), axis=0)
    hidden_rows, out_terms = together(hidden_rows, out_terms)

    grad_mixture = dot(hidden_rows, out_whole[:, :256]).astype(LOW)
    grad_heads = jnp.stack((grad_mixture[:, :128], other_core(grad_mixture[:, 128:])))
    grad_out_w = dot(hidden_rows, mixture_rows, 0, 0).astype(LOW)
    grad_out_w = grad_out_w.reshape(2, 4, 2, 64, 256)
    out_mine, out_gone = pick(grad_out_w, core, 2), pick(grad_out_w, 1 - core, 2)
    out_got = other_core(out_gone)
    out_sum = jnp.concatenate(
        (added([out_mine[..., :128], out_got[..., 128:]]), added([out_mine[..., 128:], out_got[..., :128]])), axis=2
    ).astype(LOW)

    vectors = jnp.concatenate((column_sums(hidden_rows), column_sums(cot_rows), jnp.sum(grad_pre, axis=0)[None]))
    vectors = jnp.concatenate((vectors[:, :512], vectors[:, 512:])).astype(LOW)

    grad_heads, out_sum, vectors = together(grad_heads, out_sum, vectors)
    grad_qkv = attend_backward(ids, qkv, log_totals, grad_heads.reshape(8, 128, 128))
    grad_halves = grad_qkv.reshape(2, ROWS, 384)
    gq_got = other_core(grad_halves[1])

    grad_qkv_w = dot(normed_rows, grad_halves[0], 0, 0) + dot(normed_other, grad_halves[1], 0, 0)
    gq_sums = column_sums(grad_qkv.reshape(1024, 384))
    gq_high = gq_sums.astype(LOW)
    gq_rest = (gq_sums - gq_high.astype(F32)).astype(LOW)
    grad_ln1_shift = dot(jnp.concatenate((gq_high, gq_rest)), qkv_own, 1, 1).sum(axis=0, keepdims=True)
    terms = (qkv_own.astype(F32) * grad_qkv_w).astype(LOW)
    grad_ln1_gain = (dot(jnp.ones((1, 384), LOW), terms, 1, 1) - ln1_bias * grad_ln1_shift) / ln1_gain
    ln1_sums = jnp.concatenate((grad_ln1_gain, grad_ln1_shift, grad_ln2_gain, grad_ln2_shift))
    ln1_sums, gq_got = together(ln1_sums, gq_got)
    ln1_parts = [ln1_sums] + [x_sent(ln1_sums, k) for k in (2, 1, 3)]
    back_one = (dot(grad_halves[0], qkv_own, 1, 1) + dot(gq_got, qkv_other, 1, 1)).astype(LOW)
    back_one = jnp.concatenate((back_one.reshape(4, 128, 1024), out_terms.reshape(4, 128, 1024)), axis=1)
    back_one = x_back(back_one)
    ln1_sums = added(ln1_parts)
    qv_sums = jnp.concatenate((gq_sums[:, :128], gq_sums[:, 256:]), axis=1)
    qv_sums = jnp.concatenate((jnp.where(first_core, qv_sums, 0.0), jnp.where(first_core, 0.0, qv_sums)), axis=1)
    late = jnp.concatenate((ln1_sums[:, :512], ln1_sums[:, 512:], qv_sums, jnp.zeros((1, 512), F32))).astype(LOW)
    vectors = jnp.concatenate((late, vectors))

    both = jnp.concatenate((out_sum, grad_qkv_w.astype(LOW).reshape(2, 4, 128, 384)), axis=3)
    both = jnp.concatenate((both, jnp.broadcast_to(vectors, (2, 4, 16, 512))), axis=2)
    both = lax.all_to_all(both.reshape(8, 144, 512), "dp", 0, 0, axis_index_groups=SAME_CORE, tiled=True)
    both = jnp.sum(both.astype(F32), axis=0).astype(LOW)
    both = jnp.concatenate((both, wide[:, :512], wide[:, 512:]), axis=0)
    both = added([both, lax.ppermute(both, "context", PAIR)])
    wide = jnp.concatenate((both[144:272], both[272:]), axis=1)
    both = both[:144]
    back_one = added(back_one)
    grad_norm_one = norm_backward(back_one[:128], normal_one[:128], factor_one[:128], ln1_gain)
    results = jnp.concatenate((hidden[:128] + back_one[128:] + proj_bias, grad_hidden + grad_norm_one), axis=0)
    results = swapped(results.astype(LOW))
    output, grad_tokens = results[:128][None], results[128:][None]
    fc_total, proj_total = wide[:64], wide[64:].T
    gone = jnp.concatenate((lax.dynamic_slice_in_dim(both, (1 - core) * 64, 64, 0), both[128:]), axis=0)
    got = other_core(gone)
    out_sum, vectors = both[:128, :128], both[128:] + got[64:]
    qkv_mine = lax.dynamic_slice_in_dim(both, core * 64, 64, 0)[:, 128:].reshape(64, 3, 128)
    qkv_got = got[:64, 128:].reshape(64, 3, 128)
    qkv_total = jnp.concatenate(
        (jnp.where(first_core, qkv_mine, qkv_got), jnp.where(first_core, qkv_got, qkv_mine)), axis=-1
    ).transpose(1, 0, 2)
    out_total = jnp.concatenate(
        (jnp.where(first_core, out_sum[:64], out_sum[64:]), jnp.where(first_core, out_sum[64:], out_sum[:64])), axis=1
    ).T
    norm_sums, qv_total = jnp.concatenate((vectors[0:4], vectors[4:8]), axis=1), vectors[8]
    vectors = jnp.concatenate((vectors[10:13], vectors[13:16]), axis=1)

    return (
        output,
        grad_tokens,
        norm_sums[0],
        norm_sums[1],
        qkv_total,
        qv_total.reshape(2, 2, 128).transpose(1, 0, 2).reshape(2, 256),
        out_total,
        vectors[0],
        norm_sums[2],
        norm_sums[3],
        fc_total,
        vectors[2],
        proj_total,
        vectors[1],
    )


def solution(mesh):
    in_specs = (
        P("dp", ("context", "tensor"), None),
        P(),
        P(),
        P(None, "dp", "tensor"),
        P(None, "tensor"),
        P("tensor", "dp"),
        P(),
        P(),
        P(),
        P("dp", "tensor"),
        P("tensor"),
        P("tensor", "dp"),
        P(),
        P("dp", ("context", "tensor"), None),
    )
    out_specs = (
        P("dp", ("context", "tensor"), None),
        P("dp", ("context", "tensor"), None),
        P(),
        P(),
        P(None, "dp", "tensor"),
        P(None, "tensor"),
        P("tensor", "dp"),
        P(),
        P(),
        P(),
        P("dp", "tensor"),
        P("tensor"),
        P("tensor", "dp"),
        P(),
    )
    return jax.shard_map(body, mesh=mesh, in_specs=in_specs, out_specs=out_specs, check_vma=False)
```

```python
from functools import partial

import jax
import jax.numpy as jnp
from jax import lax
from jax.experimental import pallas as pl
from jax.experimental.pallas import tpu as pltpu
from jax.experimental import pallas as pl
from jax.experimental.pallas import tpu as pltpu
from jax.experimental import pallas as pl
from jax.experimental.pallas import tpu as pltpu
from jax.experimental import pallas as pl
from jax.experimental.pallas import tpu as pltpu
from jax.experimental import pallas as pl
from jax.experimental.pallas import tpu as pltpu
from jax.experimental import pallas as pl
from jax.experimental.pallas import tpu as pltpu
from jax.experimental import pallas as pl
from jax.experimental.pallas import tpu as pltpu
from jax.experimental import pallas as pl
from jax.experimental.pallas import tpu as pltpu
from jax.experimental import pallas as pl
from jax.experimental.pallas import tpu as pltpu
from jax.experimental import pallas as pl
from jax.experimental.pallas import tpu as pltpu
from jax.experimental import pallas as pl
from jax.experimental.pallas import tpu as pltpu
from jax.experimental import pallas as pl
from jax.experimental.pallas import tpu as pltpu
from jax.experimental import pallas as pl
from jax.experimental.pallas import tpu as pltpu
from jax.experimental import pallas as pl
from jax.experimental.pallas import tpu as pltpu
from jax.experimental import pallas as pl
from jax.experimental.pallas import tpu as pltpu
from jax.experimental import pallas as pl
from jax.experimental.pallas import tpu as pltpu
from jax.experimental import pallas as pl
from jax.experimental.pallas import tpu as pltpu
from jax.experimental import pallas as pl
from jax.experimental.pallas import tpu as pltpu
from jax.experimental import pallas as pl
from jax.experimental.pallas import tpu as pltpu
from jax.sharding import PartitionSpec as P

HEAD_DIM = 64
F32 = jnp.float32
LOW = jnp.bfloat16

CORE = [(i, i ^ 1) for i in range(16)]
PAIR = [(0, 1), (1, 0)]
SAME_CORE = [[i + core for i in range(0, 16, 2)] for core in range(2)]
ROWS = 512
TILE = 256


def x_shift(k):
    return [(i, (i + k) % 4) for i in range(4)]


def swap_shift(k):
    pairs = []
    for q in range(8):
        for c in range(2):
            for h in range(2):
                for x in range(4):
                    pairs.append((((q * 2 + c) * 2 + h) * 4 + x, ((q * 2 + h) * 2 + c) * 4 + (x + k) % 4))
    return pairs


def swapped(array, k=0):
    return lax.ppermute(array, ("dp", "context", "tensor"), swap_shift(k))


def other_core(array):
    return lax.ppermute(array, "dp", CORE)


def x_sent(array, k):
    return lax.ppermute(array, "tensor", x_shift(k))


def x_parts(array):
    far = x_sent(array, 2)
    right = x_sent(array, 1)
    left = x_sent(array, 3)
    return [array, right, far, left]


def x_back(parts):
    far = x_sent(parts[2], 2)
    right = x_sent(parts[1], 3)
    left = x_sent(parts[3], 1)
    return [parts[0], right, far, left]


def pick(array, place, dim=0):
    return lax.dynamic_index_in_dim(array, place, dim, keepdims=False)


def added(parts):
    total = parts[0].astype(F32)
    for part in parts[1:]:
        total = total + part.astype(F32)
    return total


def summed_over_dp(array):
    return lax.psum_scatter(array, "dp", scatter_dimension=0, axis_index_groups=SAME_CORE, tiled=True)


def norm_forward(values_in, norm_gain, norm_bias):
    average = jnp.mean(values_in, axis=-1, keepdims=True)
    centred = values_in - average
    spread = jnp.mean(centred * centred, axis=-1, keepdims=True)
    factor = lax.rsqrt(spread + 1e-05)
    normal = centred * factor
    return (normal * norm_gain + norm_bias, normal, factor)


def norm_backward(grad_norm, normal, factor, norm_gain):
    scaled = grad_norm * norm_gain
    first_term = jnp.mean(scaled, axis=-1, keepdims=True)
    second = jnp.mean(scaled * normal, axis=-1, keepdims=True)
    return factor * (scaled - first_term - normal * second)


def gelu_and_slope(values_in):
    root = (2.0 / jnp.pi) ** 0.5
    squared = values_in * values_in
    bent = jnp.tanh(root * values_in * (1.0 + 0.044715 * squared))
    part = 0.5 * (1.0 + bent)
    slope = part + 0.5 * values_in * (1.0 - bent * bent) * root * (1.0 + 3.0 * 0.044715 * squared)
    return values_in * part, slope


def together(*arrays):
    return lax.optimization_barrier(arrays)


def dot(left, right, left_dim=1, right_dim=0):
    return lax.dot_general(left, right, (((left_dim,), (right_dim,)), ((), ())), preferred_element_type=F32)


def exact_dot(left, right):
    return lax.dot_general(left, right, (((1,), (1,)), ((), ())), precision=lax.Precision.HIGHEST, preferred_element_type=F32)


def column_sums(array):
    return dot(jnp.ones((1, array.shape[0]), array.dtype), array)


def place_of(ids, chunk):
    return (chunk // 4 ^ ids[0]) * 4 + lax.rem(ids[1] + 4 - chunk % 4, 4)


def head_lanes(rows, head):
    lanes = lax.broadcasted_iota(jnp.int32, (rows, 2 * HEAD_DIM), 1)
    return lanes < HEAD_DIM if head == 0 else lanes >= HEAD_DIM


def collect(ids, qkv, queries, keys, values):
    for chunk in range(8):
        rows = slice(chunk * 128, chunk * 128 + 128)
        place = place_of(ids, chunk)
        queries[rows] = qkv[place, :, 0:128] * jnp.asarray(HEAD_DIM**-0.5, LOW)
        keys[rows] = qkv[place, :, 128:256]
        values[rows] = qkv[place, :, 256:384]


def visible_tile():
    key_place = lax.broadcasted_iota(jnp.int32, (TILE, TILE), 0)
    return key_place <= lax.broadcasted_iota(jnp.int32, (TILE, TILE), 1)


def forward_kernel(ids, qkv, mixture, totals, queries, keys, values, mixed):
    collect(ids, qkv, queries, keys, values)
    turned = values[...].T
    for block in range(1024 // TILE):
        rows = slice(block * TILE, block * TILE + TILE)
        before = block * TILE
        kept = []
        for head in range(2):
            row_block = jnp.where(head_lanes(TILE, head), queries[rows], jnp.zeros((), LOW))
            edge = dot(keys[rows], row_block, 1, 1)
            edge = jnp.where(visible_tile(), edge, -1e30)
            largest = jnp.max(edge, axis=0, keepdims=True)
            if before:
                early = dot(keys[:before], row_block, 1, 1)
                largest = jnp.maximum(largest, jnp.max(early, axis=0, keepdims=True))
            powers = jnp.exp(edge - largest)
            summed = jnp.sum(powers, axis=0, keepdims=True)
            mix = dot(turned[:, rows], powers.astype(LOW))
            if before:
                powers = jnp.exp(early - largest)
                summed = summed + jnp.sum(powers, axis=0, keepdims=True)
                mix = mix + dot(turned[:, :before], powers.astype(LOW))
            kept.append(mix / summed)
            totals[head : head + 1, rows] = largest + jnp.log(summed)
        features = lax.broadcasted_iota(jnp.int32, (128, TILE), 0)
        mixed[rows] = jnp.where(features < HEAD_DIM, kept[0], kept[1]).T.astype(LOW)
    for chunk in range(8):
        mixture[place_of(ids, chunk)] = mixed[chunk * 128 : chunk * 128 + 128]


def backward_kernel(
    ids, qkv, totals, grad, grad_qkv, queries, keys, values, grads, grad_queries, grad_keys, grad_values
):
    collect(ids, qkv, queries, keys, values)
    for chunk in range(8):
        grads[chunk * 128 : chunk * 128 + 128] = grad[place_of(ids, chunk)]
    turned = keys[...].T
    for block in reversed(range(1024 // TILE)):
        rows = slice(block * TILE, block * TILE + TILE)
        before = block * TILE
        pieces = [rows, slice(0, before)] if before else [rows]
        sent = []
        for head in range(2):
            lanes = head_lanes(TILE, head)
            row_block = jnp.where(lanes, queries[rows], jnp.zeros((), LOW))
            grad_block = jnp.where(lanes, grads[rows], jnp.zeros((), LOW))
            total = totals[head : head + 1, rows]
            weights, products = [], []
            balance = jnp.zeros((1, TILE), F32)
            for piece in pieces:
                scores = dot(keys[piece], row_block, 1, 1)
                if piece is rows:
                    scores = jnp.where(visible_tile(), scores, -1e30)
                weight = jnp.exp(scores - total)
                product = dot(values[piece], grad_block, 1, 1)
                balance = balance + jnp.sum(weight * product, axis=0, keepdims=True)
                weights.append(weight)
                products.append(product)
            turned_grad = jnp.zeros((128, TILE), F32)
            for piece, weight, product in zip(pieces, weights, products):
                low = (weight * (product - balance)).astype(LOW)
                value_part = dot(weight.astype(LOW), grad_block)
                key_part = dot(low, row_block)
                if block == 1024 // TILE - 1 and head == 0:
                    grad_values[piece] = value_part
                    grad_keys[piece] = key_part
                else:
                    grad_values[piece] += value_part
                    grad_keys[piece] += key_part
                turned_grad = turned_grad + dot(turned[:, piece], low)
            sent.append(turned_grad)
        features = lax.broadcasted_iota(jnp.int32, (128, TILE), 0)
        grad_queries[rows] = jnp.where(features < HEAD_DIM, sent[0], sent[1]).T * HEAD_DIM**-0.5
    for chunk in range(8):
        rows = slice(chunk * 128, chunk * 128 + 128)
        place = place_of(ids, chunk)
        grad_qkv[place, :, 0:128] = grad_queries[rows].astype(LOW)
        grad_qkv[place, :, 128:256] = grad_keys[rows].astype(LOW)
        grad_qkv[place, :, 256:384] = grad_values[rows].astype(LOW)


SMEM = pl.BlockSpec(memory_space=pltpu.SMEM)
VMEM = pl.BlockSpec(memory_space=pltpu.VMEM)


def attend_forward(ids, qkv):
    return pl.pallas_call(
        forward_kernel,
        out_shape=(jax.ShapeDtypeStruct((8, 128, 128), LOW), jax.ShapeDtypeStruct((2, 1024), F32)),
        in_specs=[SMEM, VMEM],
        out_specs=(VMEM, VMEM),
        scratch_shapes=[pltpu.VMEM((1024, 128), LOW) for _ in range(4)],
        compiler_params=pltpu.CompilerParams(vmem_limit_bytes=8 * 2**20),
        cost_estimate=pl.CostEstimate(flops=700 * 2**20, bytes_accessed=2 * 2**20, transcendentals=2**20),
        name="attend_forward",
    )(ids, qkv)


def attend_backward(ids, qkv, totals, grad):
    return pl.pallas_call(
        backward_kernel,
        out_shape=jax.ShapeDtypeStruct((8, 128, 384), LOW),
        in_specs=[SMEM, VMEM, VMEM, VMEM],
        out_specs=VMEM,
        scratch_shapes=[pltpu.VMEM((1024, 128), LOW) for _ in range(4)]
        + [pltpu.VMEM((1024, 128), F32) for _ in range(3)],
        compiler_params=pltpu.CompilerParams(vmem_limit_bytes=12 * 2**20),
        cost_estimate=pl.CostEstimate(flops=1800 * 2**20, bytes_accessed=3 * 2**20, transcendentals=2**20),
        name="attend_backward",
    )(ids, qkv, totals, grad)


def body(
    tokens,
    ln1_gain,
    ln1_bias,
    qkv_weight,
    qv_bias,
    out_weight,
    out_bias,
    ln2_gain,
    ln2_bias,
    fc_weight,
    hidden_unit_bias,
    proj_weight,
    proj_bias,
    cotangent,
):
    dp = lax.axis_index("dp")
    core = dp % 2
    x = lax.axis_index("tensor")
    first_core = core == 0
    ids = jnp.stack((core, x)).astype(jnp.int32)

    token_parts = x_parts(swapped(tokens[0]))
    cot_own = swapped(cotangent[0])
    cot_rows = jnp.concatenate(x_parts(cot_own), axis=0)

    shard = qkv_weight.reshape(3, 64, 2, 128).transpose(1, 2, 0, 3).reshape(64, 768)
    line = lax.all_gather(jnp.concatenate((shard, out_weight.T), axis=1), "dp", axis=0, tiled=True)

    token_rows = jnp.concatenate(token_parts, axis=0)
    inputs = token_rows.astype(F32)
    normed_one, normal_one, factor_one = norm_forward(inputs, ln1_gain, ln1_bias)
    shard = jnp.concatenate((fc_weight, proj_weight.T), axis=1)
    cot_sums = column_sums(cot_rows)
    normed_rows, shard, cot_rows, cot_sums = together(normed_one.astype(LOW), shard, cot_rows, cot_sums)
    shard, line = together(shard, line)
    packed = lax.all_gather(shard, "dp", axis=0, tiled=True)
    fc_whole, proj_whole = packed[:, :1024], packed[:, 1024:]
    normed_other = other_core(normed_rows)
    grad_output = cot_own.astype(F32)

    qkv_own = lax.dynamic_slice_in_dim(line, core * 384, 384, 1)
    qkv_other = lax.dynamic_slice_in_dim(line, 384 - core * 384, 384, 1)
    out_own = lax.dynamic_slice_in_dim(line, 768 + core * 128, 128, 1)
    out_other = lax.dynamic_slice_in_dim(line, 896 - core * 128, 128, 1)

    shift = jnp.where(first_core, qv_bias[:, :128], qv_bias[:, 128:])
    shift = jnp.concatenate((shift[0], jnp.zeros_like(shift[0]), shift[1]))
    qkv = jnp.concatenate(
        ((dot(normed_rows, qkv_own) + shift).astype(LOW), (dot(normed_other, qkv_own) + shift).astype(LOW)), axis=0
    ).reshape(8, 128, 384)
    qkv, out_own = together(qkv, out_own)
    out_parts = x_parts(out_own)
    mixture_heads, log_totals = attend_forward(ids, qkv)
    mixture_heads = mixture_heads.reshape(2, ROWS, 128)
    mixture_rows = jnp.concatenate((mixture_heads[0], other_core(mixture_heads[1])), axis=1)
    mixture_parts = x_parts(mixture_rows)

    out_others = [out_other] + [other_core(part) for part in out_parts[1:]]
    out_whole = jnp.concatenate([part for both in zip(out_parts, out_others) for part in both], axis=1)
    mixture = jnp.concatenate([jnp.roll(mixture_parts[k], 128 * k, 0) for k in range(4)], axis=1)
    hidden = inputs + dot(mixture, out_whole, 1, 1) + out_bias
    normed_two, normal_two, factor_two = norm_forward(hidden, ln2_gain, ln2_bias)
    two_rows = normed_two.astype(LOW)

    pre_active = dot(two_rows, fc_whole) + hidden_unit_bias
    active, slope = gelu_and_slope(pre_active)
    active, slope = together(active.astype(LOW), slope)
    grad_active = dot(cot_rows, proj_whole)
    grad_pre = slope * grad_active
    grad_pre_low = grad_pre.astype(LOW)
    back_terms = dot(grad_pre_low, fc_whole, 1, 1).astype(LOW)

    back_parts = x_back(back_terms.reshape(4, 128, 1024))
    back_two = added(back_parts)
    grad_fc_w = dot(two_rows, grad_pre_low, 0, 0).astype(LOW).reshape(2, 4, 2, 64, 1024)
    grad_proj_w = dot(cot_rows, active, 0, 0).astype(LOW).reshape(2, 4, 2, 64, 1024)
    gone = jnp.concatenate((pick(grad_fc_w, 1 - core, 2), pick(grad_proj_w, 1 - core, 2)), axis=2)
    mine = jnp.concatenate((pick(grad_fc_w, core, 2), pick(grad_proj_w, core, 2)), axis=2)
    wide = added([mine, other_core(gone)]).astype(LOW)
    out_terms = dot(active, proj_whole, 1, 1).astype(LOW)

    normal_own, factor_own = normal_two[:128], factor_two[:128]
    grad_ln2_gain = jnp.sum(back_two * normal_own, axis=0, keepdims=True)
    grad_ln2_shift = jnp.sum(back_two, axis=0, keepdims=True)
    grad_hidden = grad_output + norm_backward(back_two, normal_own, factor_own, ln2_gain)

    hidden_rows = jnp.concatenate(x_parts(grad_hidden.astype(LOW)), axis=0)
    hidden_rows, out_terms = together(hidden_rows, out_terms)

    grad_mixture = dot(hidden_rows, out_whole[:, :256]).astype(LOW)
    grad_heads = jnp.stack((grad_mixture[:, :128], other_core(grad_mixture[:, 128:])))
    grad_out_w = dot(hidden_rows, mixture_rows, 0, 0).astype(LOW)
    grad_out_w = grad_out_w.reshape(2, 4, 2, 64, 256)
    out_mine, out_gone = pick(grad_out_w, core, 2), pick(grad_out_w, 1 - core, 2)
    out_got = other_core(out_gone)
    out_sum = jnp.concatenate(
        (added([out_mine[..., :128], out_got[..., 128:]]), added([out_mine[..., 128:], out_got[..., :128]])), axis=2
    ).astype(LOW)

    vectors = jnp.concatenate((column_sums(hidden_rows), cot_sums, jnp.sum(grad_pre, axis=0)[None]))
    vectors = jnp.concatenate((vectors[:, :512], vectors[:, 512:])).astype(LOW)

    grad_heads, out_sum, vectors, wide = together(grad_heads, out_sum, vectors, wide)
    wide = summed_over_dp(wide.reshape(1024, 1024))
    grad_qkv = attend_backward(ids, qkv, log_totals, grad_heads.reshape(8, 128, 128))
    grad_halves = grad_qkv.reshape(2, ROWS, 384)
    gq_got = other_core(grad_halves[1])

    grad_qkv_w = dot(normed_rows, grad_halves[0], 0, 0) + dot(normed_other, grad_halves[1], 0, 0)
    gq_sums = column_sums(grad_qkv.reshape(1024, 384))
    gq_high = gq_sums.astype(LOW)
    gq_rest = (gq_sums - gq_high.astype(F32)).astype(LOW)
    grad_ln1_shift = dot(jnp.concatenate((gq_high, gq_rest)), qkv_own, 1, 1).sum(axis=0, keepdims=True)
    terms = (qkv_own.astype(F32) * grad_qkv_w).astype(LOW)
    grad_ln1_gain = (dot(jnp.ones((1, 384), LOW), terms, 1, 1) - ln1_bias * grad_ln1_shift) / ln1_gain
    ln1_sums = jnp.concatenate((grad_ln1_gain, grad_ln1_shift, grad_ln2_gain, grad_ln2_shift))
    ln1_sums, gq_got = together(ln1_sums, gq_got)
    ln1_parts = [ln1_sums] + [x_sent(ln1_sums, k) for k in (2, 1, 3)]
    back_one = (dot(grad_halves[0], qkv_own, 1, 1) + dot(gq_got, qkv_other, 1, 1)).astype(LOW)
    back_one = jnp.concatenate((back_one.reshape(4, 128, 1024), out_terms.reshape(4, 128, 1024)), axis=1)
    back_one = x_back(back_one)
    ln1_sums = added(ln1_parts)
    qv_sums = jnp.concatenate((gq_sums[:, :128], gq_sums[:, 256:]), axis=1)
    qv_sums = jnp.concatenate((jnp.where(first_core, qv_sums, 0.0), jnp.where(first_core, 0.0, qv_sums)), axis=1)
    late = jnp.concatenate((ln1_sums[:, :512], ln1_sums[:, 512:], qv_sums, jnp.zeros((1, 512), F32))).astype(LOW)
    vectors = jnp.concatenate((late, vectors))

    both = jnp.concatenate((out_sum, grad_qkv_w.astype(LOW).reshape(2, 4, 128, 384)), axis=3)
    both = jnp.concatenate((both, jnp.broadcast_to(vectors, (2, 4, 16, 512))), axis=2)
    both = lax.all_to_all(both.reshape(8, 144, 512), "dp", 0, 0, axis_index_groups=SAME_CORE, tiled=True)
    both = jnp.sum(both.astype(F32), axis=0).astype(LOW)
    both = jnp.concatenate((both, wide[:, :512], wide[:, 512:]), axis=0)
    both = added([both, lax.ppermute(both, "context", PAIR)])
    wide = jnp.concatenate((both[144:272], both[272:]), axis=1)
    both = both[:144]
    back_one = added(back_one)
    grad_norm_one = norm_backward(back_one[:128], normal_one[:128], factor_one[:128], ln1_gain)
    results = jnp.concatenate((hidden[:128] + back_one[128:] + proj_bias, grad_hidden + grad_norm_one), axis=0)
    results = swapped(results.astype(LOW))
    output, grad_tokens = results[:128][None], results[128:][None]
    fc_total, proj_total = wide[:64], wide[64:].T
    gone = jnp.concatenate((lax.dynamic_slice_in_dim(both, (1 - core) * 64, 64, 0), both[128:]), axis=0)
    got = other_core(gone)
    out_sum, vectors = both[:128, :128], both[128:] + got[64:]
    qkv_mine = lax.dynamic_slice_in_dim(both, core * 64, 64, 0)[:, 128:].reshape(64, 3, 128)
    qkv_got = got[:64, 128:].reshape(64, 3, 128)
    qkv_total = jnp.concatenate(
        (jnp.where(first_core, qkv_mine, qkv_got), jnp.where(first_core, qkv_got, qkv_mine)), axis=-1
    ).transpose(1, 0, 2)
    out_total = jnp.concatenate(
        (jnp.where(first_core, out_sum[:64], out_sum[64:]), jnp.where(first_core, out_sum[64:], out_sum[:64])), axis=1
    ).T
    norm_sums, qv_total = jnp.concatenate((vectors[0:4], vectors[4:8]), axis=1), vectors[8]
    vectors = jnp.concatenate((vectors[10:13], vectors[13:16]), axis=1)

    return (
        output,
        grad_tokens,
        norm_sums[0],
        norm_sums[1],
        qkv_total,
        qv_total.reshape(2, 2, 128).transpose(1, 0, 2).reshape(2, 256),
        out_total,
        vectors[0],
        norm_sums[2],
        norm_sums[3],
        fc_total,
        vectors[2],
        proj_total,
        vectors[1],
    )


def solution(mesh):
    in_specs = (
        P("dp", ("context", "tensor"), None),
        P(),
        P(),
        P(None, "dp", "tensor"),
        P(None, "tensor"),
        P("tensor", "dp"),
        P(),
        P(),
        P(),
        P("dp", "tensor"),
        P("tensor"),
        P("tensor", "dp"),
        P(),
        P("dp", ("context", "tensor"), None),
    )
    out_specs = (
        P("dp", ("context", "tensor"), None),
        P("dp", ("context", "tensor"), None),
        P(),
        P(),
        P(None, "dp", "tensor"),
        P(None, "tensor"),
        P("tensor", "dp"),
        P(),
        P(),
        P(),
        P("dp", "tensor"),
        P("tensor"),
        P("tensor", "dp"),
        P(),
    )
    return jax.shard_map(body, mesh=mesh, in_specs=in_specs, out_specs=out_specs, check_vma=False)
```

```python
from functools import partial

import jax
import jax.numpy as jnp
from jax import lax
from jax.experimental import pallas as pl
from jax.experimental.pallas import tpu as pltpu
from jax.experimental import pallas as pl
from jax.experimental.pallas import tpu as pltpu
from jax.experimental import pallas as pl
from jax.experimental.pallas import tpu as pltpu
from jax.experimental import pallas as pl
from jax.experimental.pallas import tpu as pltpu
from jax.experimental import pallas as pl
from jax.experimental.pallas import tpu as pltpu
from jax.experimental import pallas as pl
from jax.experimental.pallas import tpu as pltpu
from jax.experimental import pallas as pl
from jax.experimental.pallas import tpu as pltpu
from jax.experimental import pallas as pl
from jax.experimental.pallas import tpu as pltpu
from jax.experimental import pallas as pl
from jax.experimental.pallas import tpu as pltpu
from jax.experimental import pallas as pl
from jax.experimental.pallas import tpu as pltpu
from jax.experimental import pallas as pl
from jax.experimental.pallas import tpu as pltpu
from jax.experimental import pallas as pl
from jax.experimental.pallas import tpu as pltpu
from jax.experimental import pallas as pl
from jax.experimental.pallas import tpu as pltpu
from jax.experimental import pallas as pl
from jax.experimental.pallas import tpu as pltpu
from jax.experimental import pallas as pl
from jax.experimental.pallas import tpu as pltpu
from jax.experimental import pallas as pl
from jax.experimental.pallas import tpu as pltpu
from jax.experimental import pallas as pl
from jax.experimental.pallas import tpu as pltpu
from jax.experimental import pallas as pl
from jax.experimental.pallas import tpu as pltpu
from jax.experimental import pallas as pl
from jax.experimental.pallas import tpu as pltpu
from jax.sharding import PartitionSpec as P

HEAD_DIM = 64
F32 = jnp.float32
LOW = jnp.bfloat16

CORE = [(i, i ^ 1) for i in range(16)]
PAIR = [(0, 1), (1, 0)]
SAME_CORE = [[i + core for i in range(0, 16, 2)] for core in range(2)]
ROWS = 512
TILE = 256


def x_shift(k):
    return [(i, (i + k) % 4) for i in range(4)]


def swap_shift(k):
    pairs = []
    for q in range(8):
        for c in range(2):
            for h in range(2):
                for x in range(4):
                    pairs.append((((q * 2 + c) * 2 + h) * 4 + x, ((q * 2 + h) * 2 + c) * 4 + (x + k) % 4))
    return pairs


def swapped(array, k=0):
    return lax.ppermute(array, ("dp", "context", "tensor"), swap_shift(k))


def other_core(array):
    return lax.ppermute(array, "dp", CORE)


def x_sent(array, k):
    return lax.ppermute(array, "tensor", x_shift(k))


def x_parts(array):
    far = x_sent(array, 2)
    right = x_sent(array, 1)
    left = x_sent(array, 3)
    return [array, right, far, left]


def x_back(parts):
    far = x_sent(parts[2], 2)
    right = x_sent(parts[1], 3)
    left = x_sent(parts[3], 1)
    return [parts[0], right, far, left]


def pick(array, place, dim=0):
    return lax.dynamic_index_in_dim(array, place, dim, keepdims=False)


def added(parts):
    total = parts[0].astype(F32)
    for part in parts[1:]:
        total = total + part.astype(F32)
    return total


def summed_over_dp(array):
    return lax.psum_scatter(array, "dp", scatter_dimension=0, axis_index_groups=SAME_CORE, tiled=True)


def norm_forward(values_in, norm_gain, norm_bias):
    average = jnp.mean(values_in, axis=-1, keepdims=True)
    centred = values_in - average
    spread = jnp.mean(centred * centred, axis=-1, keepdims=True)
    factor = lax.rsqrt(spread + 1e-05)
    normal = centred * factor
    return (normal * norm_gain + norm_bias, normal, factor)


def norm_backward(grad_norm, normal, factor, norm_gain):
    scaled = grad_norm * norm_gain
    first_term = jnp.mean(scaled, axis=-1, keepdims=True)
    second = jnp.mean(scaled * normal, axis=-1, keepdims=True)
    return factor * (scaled - first_term - normal * second)


def gelu_and_slope(values_in):
    root = (2.0 / jnp.pi) ** 0.5
    squared = values_in * values_in
    bent = jnp.tanh(values_in * (root + root * 0.044715 * squared))
    part = 0.5 + 0.5 * bent
    result = values_in * part
    slope = part + result * (1.0 - bent) * (root + 3.0 * root * 0.044715 * squared)
    return result, slope


def together(*arrays):
    return lax.optimization_barrier(arrays)


def dot(left, right, left_dim=1, right_dim=0):
    return lax.dot_general(left, right, (((left_dim,), (right_dim,)), ((), ())), preferred_element_type=F32)


def exact_dot(left, right):
    return lax.dot_general(left, right, (((1,), (1,)), ((), ())), precision=lax.Precision.HIGHEST, preferred_element_type=F32)


def column_sums(array):
    return dot(jnp.ones((1, array.shape[0]), array.dtype), array)


def place_of(ids, chunk):
    return (chunk // 4 ^ ids[0]) * 4 + lax.rem(ids[1] + 4 - chunk % 4, 4)


def head_lanes(rows, head):
    lanes = lax.broadcasted_iota(jnp.int32, (rows, 2 * HEAD_DIM), 1)
    return lanes < HEAD_DIM if head == 0 else lanes >= HEAD_DIM


def collect(ids, qkv, queries, keys, values):
    for chunk in range(8):
        rows = slice(chunk * 128, chunk * 128 + 128)
        place = place_of(ids, chunk)
        queries[rows] = qkv[place, :, 0:128] * jnp.asarray(HEAD_DIM**-0.5, LOW)
        keys[rows] = qkv[place, :, 128:256]
        values[rows] = qkv[place, :, 256:384]


def visible_tile():
    key_place = lax.broadcasted_iota(jnp.int32, (TILE, TILE), 0)
    return key_place <= lax.broadcasted_iota(jnp.int32, (TILE, TILE), 1)


def forward_kernel(ids, qkv, mixture, totals, queries, keys, values, mixed):
    collect(ids, qkv, queries, keys, values)
    turned = values[...].T
    for block in range(1024 // TILE):
        rows = slice(block * TILE, block * TILE + TILE)
        before = block * TILE
        kept = []
        for head in range(2):
            row_block = jnp.where(head_lanes(TILE, head), queries[rows], jnp.zeros((), LOW))
            edge = dot(keys[rows], row_block, 1, 1)
            edge = jnp.where(visible_tile(), edge, -1e30)
            largest = jnp.max(edge, axis=0, keepdims=True)
            if before:
                early = dot(keys[:before], row_block, 1, 1)
                largest = jnp.maximum(largest, jnp.max(early, axis=0, keepdims=True))
            powers = jnp.exp(edge - largest)
            summed = jnp.sum(powers, axis=0, keepdims=True)
            mix = dot(turned[:, rows], powers.astype(LOW))
            if before:
                powers = jnp.exp(early - largest)
                summed = summed + jnp.sum(powers, axis=0, keepdims=True)
                mix = mix + dot(turned[:, :before], powers.astype(LOW))
            kept.append(mix / summed)
            totals[head : head + 1, rows] = largest + jnp.log(summed)
        features = lax.broadcasted_iota(jnp.int32, (128, TILE), 0)
        mixed[rows] = jnp.where(features < HEAD_DIM, kept[0], kept[1]).T.astype(LOW)
    for chunk in range(8):
        mixture[place_of(ids, chunk)] = mixed[chunk * 128 : chunk * 128 + 128]


def backward_kernel(
    ids, qkv, totals, grad, grad_qkv, queries, keys, values, grads, grad_queries, grad_keys, grad_values
):
    collect(ids, qkv, queries, keys, values)
    for chunk in range(8):
        grads[chunk * 128 : chunk * 128 + 128] = grad[place_of(ids, chunk)]
    turned = keys[...].T
    for block in reversed(range(1024 // TILE)):
        rows = slice(block * TILE, block * TILE + TILE)
        before = block * TILE
        pieces = [rows, slice(0, before)] if before else [rows]
        sent = []
        for head in range(2):
            lanes = head_lanes(TILE, head)
            row_block = jnp.where(lanes, queries[rows], jnp.zeros((), LOW))
            grad_block = jnp.where(lanes, grads[rows], jnp.zeros((), LOW))
            total = totals[head : head + 1, rows]
            weights, products = [], []
            balance = jnp.zeros((1, TILE), F32)
            for piece in pieces:
                scores = dot(keys[piece], row_block, 1, 1)
                if piece is rows:
                    scores = jnp.where(visible_tile(), scores, -1e30)
                weight = jnp.exp(scores - total)
                product = dot(values[piece], grad_block, 1, 1)
                balance = balance + jnp.sum(weight * product, axis=0, keepdims=True)
                weights.append(weight)
                products.append(product)
            turned_grad = jnp.zeros((128, TILE), F32)
            for piece, weight, product in zip(pieces, weights, products):
                low = (weight * (product - balance)).astype(LOW)
                value_part = dot(weight.astype(LOW), grad_block)
                key_part = dot(low, row_block)
                if block == 1024 // TILE - 1 and head == 0:
                    grad_values[piece] = value_part
                    grad_keys[piece] = key_part
                else:
                    grad_values[piece] += value_part
                    grad_keys[piece] += key_part
                turned_grad = turned_grad + dot(turned[:, piece], low)
            sent.append(turned_grad)
        features = lax.broadcasted_iota(jnp.int32, (128, TILE), 0)
        grad_queries[rows] = jnp.where(features < HEAD_DIM, sent[0], sent[1]).T * HEAD_DIM**-0.5
    for chunk in range(8):
        rows = slice(chunk * 128, chunk * 128 + 128)
        place = place_of(ids, chunk)
        grad_qkv[place, :, 0:128] = grad_queries[rows].astype(LOW)
        grad_qkv[place, :, 128:256] = grad_keys[rows].astype(LOW)
        grad_qkv[place, :, 256:384] = grad_values[rows].astype(LOW)


SMEM = pl.BlockSpec(memory_space=pltpu.SMEM)
VMEM = pl.BlockSpec(memory_space=pltpu.VMEM)


def attend_forward(ids, qkv):
    return pl.pallas_call(
        forward_kernel,
        out_shape=(jax.ShapeDtypeStruct((8, 128, 128), LOW), jax.ShapeDtypeStruct((2, 1024), F32)),
        in_specs=[SMEM, VMEM],
        out_specs=(VMEM, VMEM),
        scratch_shapes=[pltpu.VMEM((1024, 128), LOW) for _ in range(4)],
        compiler_params=pltpu.CompilerParams(vmem_limit_bytes=8 * 2**20),
        cost_estimate=pl.CostEstimate(flops=700 * 2**20, bytes_accessed=2 * 2**20, transcendentals=2**20),
        name="attend_forward",
    )(ids, qkv)


def attend_backward(ids, qkv, totals, grad):
    return pl.pallas_call(
        backward_kernel,
        out_shape=jax.ShapeDtypeStruct((8, 128, 384), LOW),
        in_specs=[SMEM, VMEM, VMEM, VMEM],
        out_specs=VMEM,
        scratch_shapes=[pltpu.VMEM((1024, 128), LOW) for _ in range(4)]
        + [pltpu.VMEM((1024, 128), F32) for _ in range(3)],
        compiler_params=pltpu.CompilerParams(vmem_limit_bytes=12 * 2**20),
        cost_estimate=pl.CostEstimate(flops=1800 * 2**20, bytes_accessed=3 * 2**20, transcendentals=2**20),
        name="attend_backward",
    )(ids, qkv, totals, grad)


def body(
    tokens,
    ln1_gain,
    ln1_bias,
    qkv_weight,
    qv_bias,
    out_weight,
    out_bias,
    ln2_gain,
    ln2_bias,
    fc_weight,
    hidden_unit_bias,
    proj_weight,
    proj_bias,
    cotangent,
):
    dp = lax.axis_index("dp")
    core = dp % 2
    x = lax.axis_index("tensor")
    first_core = core == 0
    ids = jnp.stack((core, x)).astype(jnp.int32)

    token_parts = x_parts(swapped(tokens[0]))
    cot_own = swapped(cotangent[0])
    cot_rows = jnp.concatenate(x_parts(cot_own), axis=0)

    shard = qkv_weight.reshape(3, 64, 2, 128).transpose(1, 2, 0, 3).reshape(64, 768)
    line = lax.all_gather(jnp.concatenate((shard, out_weight.T), axis=1), "dp", axis=0, tiled=True)

    token_rows = jnp.concatenate(token_parts, axis=0)
    inputs = token_rows.astype(F32)
    normed_one, normal_one, factor_one = norm_forward(inputs, ln1_gain, ln1_bias)
    shard = jnp.concatenate((fc_weight, proj_weight.T), axis=1)
    cot_sums = column_sums(cot_rows)
    normed_rows, shard, cot_rows, cot_sums = together(normed_one.astype(LOW), shard, cot_rows, cot_sums)
    shard, line = together(shard, line)
    packed = lax.all_gather(shard, "dp", axis=0, tiled=True)
    fc_whole, proj_whole = packed[:, :1024], packed[:, 1024:]
    normed_other = other_core(normed_rows)
    grad_output = cot_own.astype(F32)

    qkv_own = lax.dynamic_slice_in_dim(line, core * 384, 384, 1)
    qkv_other = lax.dynamic_slice_in_dim(line, 384 - core * 384, 384, 1)
    out_own = lax.dynamic_slice_in_dim(line, 768 + core * 128, 128, 1)
    out_other = lax.dynamic_slice_in_dim(line, 896 - core * 128, 128, 1)

    shift = jnp.where(first_core, qv_bias[:, :128], qv_bias[:, 128:])
    shift = jnp.concatenate((shift[0], jnp.zeros_like(shift[0]), shift[1]))
    qkv = jnp.concatenate(
        ((dot(normed_rows, qkv_own) + shift).astype(LOW), (dot(normed_other, qkv_own) + shift).astype(LOW)), axis=0
    ).reshape(8, 128, 384)
    qkv, out_own = together(qkv, out_own)
    out_parts = x_parts(out_own)
    mixture_heads, log_totals = attend_forward(ids, qkv)
    mixture_heads = mixture_heads.reshape(2, ROWS, 128)
    mixture_rows = jnp.concatenate((mixture_heads[0], other_core(mixture_heads[1])), axis=1)
    mixture_parts = x_parts(mixture_rows)

    out_others = [out_other] + [other_core(part) for part in out_parts[1:]]
    out_whole = jnp.concatenate([part for both in zip(out_parts, out_others) for part in both], axis=1)
    mixture = jnp.concatenate([jnp.roll(mixture_parts[k], 128 * k, 0) for k in range(4)], axis=1)
    hidden = inputs + dot(mixture, out_whole, 1, 1) + out_bias
    normed_two, normal_two, factor_two = norm_forward(hidden, ln2_gain, ln2_bias)
    two_rows = normed_two.astype(LOW)

    pre_active = dot(two_rows, fc_whole) + hidden_unit_bias
    active, slope = gelu_and_slope(pre_active)
    active, slope = together(active.astype(LOW), slope)
    grad_active = dot(cot_rows, proj_whole)
    grad_pre = slope * grad_active
    grad_pre_low = grad_pre.astype(LOW)
    back_terms = dot(grad_pre_low, fc_whole, 1, 1).astype(LOW)

    active, two_rows, back_terms = together(active, two_rows, back_terms)
    back_parts = x_back(back_terms.reshape(4, 128, 1024))
    back_two = added(back_parts)
    grad_fc_w = dot(two_rows, grad_pre_low, 0, 0).astype(LOW).reshape(2, 4, 2, 64, 1024)
    grad_proj_w = dot(cot_rows, active, 0, 0).astype(LOW).reshape(2, 4, 2, 64, 1024)
    gone = jnp.concatenate((pick(grad_fc_w, 1 - core, 2), pick(grad_proj_w, 1 - core, 2)), axis=2)
    mine = jnp.concatenate((pick(grad_fc_w, core, 2), pick(grad_proj_w, core, 2)), axis=2)
    wide = added([mine, other_core(gone)]).astype(LOW)
    out_terms = dot(active, proj_whole, 1, 1).astype(LOW)

    normal_own, factor_own = normal_two[:128], factor_two[:128]
    grad_ln2_gain = jnp.sum(back_two * normal_own, axis=0, keepdims=True)
    grad_ln2_shift = jnp.sum(back_two, axis=0, keepdims=True)
    grad_hidden = grad_output + norm_backward(back_two, normal_own, factor_own, ln2_gain)

    hidden_rows = jnp.concatenate(x_parts(grad_hidden.astype(LOW)), axis=0)
    hidden_rows, out_terms = together(hidden_rows, out_terms)

    grad_mixture = dot(hidden_rows, out_whole[:, :256]).astype(LOW)
    grad_heads = jnp.stack((grad_mixture[:, :128], other_core(grad_mixture[:, 128:])))
    grad_out_w = dot(hidden_rows, mixture_rows, 0, 0).astype(LOW)
    grad_out_w = grad_out_w.reshape(2, 4, 2, 64, 256)
    out_mine, out_gone = pick(grad_out_w, core, 2), pick(grad_out_w, 1 - core, 2)
    out_got = other_core(out_gone)
    out_sum = jnp.concatenate(
        (added([out_mine[..., :128], out_got[..., 128:]]), added([out_mine[..., 128:], out_got[..., :128]])), axis=2
    ).astype(LOW)

    vectors = jnp.concatenate((column_sums(hidden_rows), cot_sums, jnp.sum(grad_pre, axis=0)[None]))
    vectors = jnp.concatenate((vectors[:, :512], vectors[:, 512:])).astype(LOW)

    grad_heads, out_sum, vectors, wide = together(grad_heads, out_sum, vectors, wide)
    wide = summed_over_dp(wide.reshape(1024, 1024))
    grad_qkv = attend_backward(ids, qkv, log_totals, grad_heads.reshape(8, 128, 128))
    grad_halves = grad_qkv.reshape(2, ROWS, 384)
    gq_got = other_core(grad_halves[1])

    grad_qkv_w = dot(normed_rows, grad_halves[0], 0, 0) + dot(normed_other, grad_halves[1], 0, 0)
    gq_sums = column_sums(grad_qkv.reshape(1024, 384))
    gq_high = gq_sums.astype(LOW)
    gq_rest = (gq_sums - gq_high.astype(F32)).astype(LOW)
    grad_ln1_shift = dot(jnp.concatenate((gq_high, gq_rest)), qkv_own, 1, 1).sum(axis=0, keepdims=True)
    terms = (qkv_own.astype(F32) * grad_qkv_w).astype(LOW)
    grad_ln1_gain = (dot(jnp.ones((1, 384), LOW), terms, 1, 1) - ln1_bias * grad_ln1_shift) / ln1_gain
    ln1_sums = jnp.concatenate((grad_ln1_gain, grad_ln1_shift, grad_ln2_gain, grad_ln2_shift))
    ln1_sums, gq_got = together(ln1_sums, gq_got)
    ln1_parts = [ln1_sums] + [x_sent(ln1_sums, k) for k in (2, 1, 3)]
    back_one = (dot(grad_halves[0], qkv_own, 1, 1) + dot(gq_got, qkv_other, 1, 1)).astype(LOW)
    back_one = jnp.concatenate((back_one.reshape(4, 128, 1024), out_terms.reshape(4, 128, 1024)), axis=1)
    back_one = x_back(back_one)
    ln1_sums = added(ln1_parts)
    qv_sums = jnp.concatenate((gq_sums[:, :128], gq_sums[:, 256:]), axis=1)
    qv_sums = jnp.concatenate((jnp.where(first_core, qv_sums, 0.0), jnp.where(first_core, 0.0, qv_sums)), axis=1)
    late = jnp.concatenate((ln1_sums[:, :512], ln1_sums[:, 512:], qv_sums, jnp.zeros((1, 512), F32))).astype(LOW)
    vectors = jnp.concatenate((late, vectors))

    both = jnp.concatenate((out_sum, grad_qkv_w.astype(LOW).reshape(2, 4, 128, 384)), axis=3)
    both = jnp.concatenate((both, jnp.broadcast_to(vectors, (2, 4, 16, 512))), axis=2)
    both = lax.all_to_all(both.reshape(8, 144, 512), "dp", 0, 0, axis_index_groups=SAME_CORE, tiled=True)
    both = jnp.sum(both.astype(F32), axis=0).astype(LOW)
    both = jnp.concatenate((both, wide[:, :512], wide[:, 512:]), axis=0)
    both = added([both, lax.ppermute(both, "context", PAIR)])
    wide = jnp.concatenate((both[144:272], both[272:]), axis=1)
    both = both[:144]
    back_one = added(back_one)
    grad_norm_one = norm_backward(back_one[:128], normal_one[:128], factor_one[:128], ln1_gain)
    results = jnp.concatenate((hidden[:128] + back_one[128:] + proj_bias, grad_hidden + grad_norm_one), axis=0)
    results = swapped(results.astype(LOW))
    output, grad_tokens = results[:128][None], results[128:][None]
    fc_total, proj_total = wide[:64], wide[64:].T
    gone = jnp.concatenate((lax.dynamic_slice_in_dim(both, (1 - core) * 64, 64, 0), both[128:]), axis=0)
    got = other_core(gone)
    out_sum, vectors = both[:128, :128], both[128:] + got[64:]
    qkv_mine = lax.dynamic_slice_in_dim(both, core * 64, 64, 0)[:, 128:].reshape(64, 3, 128)
    qkv_got = got[:64, 128:].reshape(64, 3, 128)
    qkv_total = jnp.concatenate(
        (jnp.where(first_core, qkv_mine, qkv_got), jnp.where(first_core, qkv_got, qkv_mine)), axis=-1
    ).transpose(1, 0, 2)
    out_total = jnp.concatenate(
        (jnp.where(first_core, out_sum[:64], out_sum[64:]), jnp.where(first_core, out_sum[64:], out_sum[:64])), axis=1
    ).T
    norm_sums, qv_total = jnp.concatenate((vectors[0:4], vectors[4:8]), axis=1), vectors[8]
    vectors = jnp.concatenate((vectors[10:13], vectors[13:16]), axis=1)

    return (
        output,
        grad_tokens,
        norm_sums[0],
        norm_sums[1],
        qkv_total,
        qv_total.reshape(2, 2, 128).transpose(1, 0, 2).reshape(2, 256),
        out_total,
        vectors[0],
        norm_sums[2],
        norm_sums[3],
        fc_total,
        vectors[2],
        proj_total,
        vectors[1],
    )


def solution(mesh):
    in_specs = (
        P("dp", ("context", "tensor"), None),
        P(),
        P(),
        P(None, "dp", "tensor"),
        P(None, "tensor"),
        P("tensor", "dp"),
        P(),
        P(),
        P(),
        P("dp", "tensor"),
        P("tensor"),
        P("tensor", "dp"),
        P(),
        P("dp", ("context", "tensor"), None),
    )
    out_specs = (
        P("dp", ("context", "tensor"), None),
        P("dp", ("context", "tensor"), None),
        P(),
        P(),
        P(None, "dp", "tensor"),
        P(None, "tensor"),
        P("tensor", "dp"),
        P(),
        P(),
        P(),
        P("dp", "tensor"),
        P("tensor"),
        P("tensor", "dp"),
        P(),
    )
    return jax.shard_map(body, mesh=mesh, in_specs=in_specs, out_specs=out_specs, check_vma=False)
```
